512 devices in a mesh: band: 64 (over z, x_lo, core), lev: 8 (over y, x_hi).
Axes of the slice: x: 4 (x_hi: 2, x_lo: 2; x = x_hi * 2 + x_lo), y: 4, z: 16, core: 2. Of those that a mesh axis runs over, the one named last changes fastest.
Arguments:
- air_heat_state: bfloat16 [8, 2, 512, 4096], P('lev', None, 'band'), may hold values from -6 to 6
- mixing_coefficient: bfloat16 [2, 512, 4096], P(None, 'band'), may hold values from 0.049804688 to 0.19921875
- layer_depth_factor: float32 [8], P('lev'), may hold values from 0.3 to 0.8
- weighted_polynomial_table: bfloat16 [512, 320, 641], P('band'), may hold values from -0.5 to 0.5
- wavenumber_to_mode_degree: int32 [320], replicated, may hold values from 0 to 319, each once
Outputs:
- smoothed: bfloat16 [8, 2, 512, 4096], P('lev', None, 'band')
- spectral: float32 [8, 2, 2, 320, 641], P('lev', None, None, 'band')
The draws below stay inside these ranges and needn't reach their ends.
Inputs may be any that keep to these rules, and one draw needn't show every extreme that they name: wavenumber_to_mode_degree holds every pair row 0 to 319 once; pair row p holds wavenumbers p and 639 - p.
All inputs are finite; a program needn't handle non-finite values.
Results may differ from the reference program's by a relative error of at most 0.009.
Values may be sent and summed in bfloat16 or wider, within the bound.
A program may use at most 128 MiB of HBM per device.

```python
import math
import jax
import jax.numpy as jnp
from jax import lax

ZONAL_POINTS = 4096
MERIDIAN_STEPS = 1024
K = 640
VERTICAL_LAYERS = 8


def raised(values, own_key, source, target, blocks, factor):
    owner, partner = [(jnp.arange(values.shape[position]) // (values.shape[position] // blocks)).reshape([-1 if axis == position else 1 for axis in range(values.ndim)]) for position in (source, target)]
    chosen = jax.random.permutation(own_key, blocks)[partner]
    strong = (owner == chosen) | (owner == (partner + blocks // 2) % blocks)
    return jnp.where(strong, factor * values, values)


def levels(key, shape, pieces, least, high):
    factor_of = 1.0
    for position, blocks in pieces:
        steps = jax.random.uniform(jax.random.fold_in(jax.random.fold_in(key, 6), position), (blocks,), jnp.float32, least / len(pieces), high / len(pieces))
        factor_of = factor_of * jnp.repeat(jnp.exp(steps), shape[position] // blocks).reshape((-1,) + (1,) * (len(shape) - 1 - position))
    return factor_of


def noise(own_key, extent, scale, reach, cuts=(), held_as=jnp.bfloat16):
    gain = levels(own_key, extent, cuts, -0.22, 0.18) if cuts else 1.0
    values = jax.random.normal(own_key, extent, jnp.float32) * scale * gain
    return jnp.minimum(jnp.maximum(values, -reach), reach).astype(held_as)


def gaussian_with(key, dims, width, bound, cuts, heavy, kind=jnp.bfloat16):
    result = width * jax.random.normal(key, dims, jnp.float32)
    if cuts:
        result = result * levels(key, dims, cuts, -0.22, 0.18)
    return jnp.clip(raised(result, jax.random.fold_in(key, 3), *heavy), -bound, bound).astype(kind)


def setup_inputs(seed: int = 0) -> dict:
    streams_of = jax.random.split(jax.random.key(seed), 6)
    return {
        "air_heat_state": noise(streams_of[0], (VERTICAL_LAYERS, 2, MERIDIAN_STEPS // 2, ZONAL_POINTS), 1.0, 6.0, ((0, 8), (2, 64))),
        "mixing_coefficient": jnp.clip(jnp.exp(math.log(0.19921875) - 1.3862944 * jax.random.uniform(streams_of[1], (2, MERIDIAN_STEPS // 2, ZONAL_POINTS), jnp.float32) ** levels(streams_of[1], (2, MERIDIAN_STEPS // 2, ZONAL_POINTS), ((1, 64),), -0.2, 0.2)), 0.049804688, 0.19921875).astype(jnp.bfloat16),
        "layer_depth_factor": jnp.clip(jnp.exp(math.log(0.8) - 0.98082923 * jax.random.uniform(streams_of[2], (VERTICAL_LAYERS,), jnp.float32) ** levels(streams_of[2], (VERTICAL_LAYERS,), ((0, 8),), -0.2, 0.2)), 0.3, 0.8),
        "weighted_polynomial_table": gaussian_with(streams_of[3], (MERIDIAN_STEPS // 2, K // 2, K + 1), MERIDIAN_STEPS ** -0.5, 0.5, ((0, 64),), (0, 1, 64, 4.0)),
        "wavenumber_to_mode_degree": jax.random.permutation(streams_of[4], K // 2).astype(jnp.int32),
    }


def pair_terms(products, pair_index, columns):
    count_pairs = products.shape[0]
    products = products.reshape(count_pairs, 4, products.shape[1] // 4, columns)
    column_ids = jnp.arange(columns, dtype=jnp.int32)[None, :]
    pair_ids = pair_index.astype(jnp.int32)[:, None]
    first_part = column_ids < columns - 1 - pair_ids
    parity = jnp.where(first_part, column_ids % 2, (column_ids + pair_ids) % 2)
    signs = (1 - 2 * parity).astype(products.dtype)[:, None, :]
    first_part = first_part[:, None, :]
    return jnp.where(first_part, products[:, 0] + signs * products[:, 1], products[:, 2] + signs * products[:, 3])

def reference(air_heat_state, mixing_coefficient, layer_depth_factor, weighted_polynomial_table, wavenumber_to_mode_degree):
    half_rows = MERIDIAN_STEPS // 2
    physical_space_values = air_heat_state.astype(jnp.float32)
    kappa_field = mixing_coefficient.astype(jnp.float32)
    row_ids = jnp.arange(half_rows, dtype=jnp.float32)
    centre = jnp.sin((row_ids + 0.5) * (math.pi / MERIDIAN_STEPS))[:, None]
    upper_face = jnp.sin((row_ids + 1.0) * (math.pi / MERIDIAN_STEPS))[:, None]
    lower_face = jnp.sin(row_ids * (math.pi / MERIDIAN_STEPS))[:, None]
    eastward = jnp.roll(physical_space_values, -1, axis=3)
    westward = jnp.roll(physical_space_values, 1, axis=3)
    poleward = jnp.concatenate([jnp.zeros_like(physical_space_values[:, :, :1]), physical_space_values[:, :, :-1]], axis=2)
    equatorward = jnp.concatenate([physical_space_values[:, :, 1:], physical_space_values[:, ::-1, -1:]], axis=2)
    meridional = (upper_face * (equatorward - physical_space_values) - lower_face * (physical_space_values - poleward)) / centre
    smoothed = (physical_space_values + kappa_field[None] * (eastward - 2.0 * physical_space_values + westward + meridional)).astype(jnp.bfloat16)
    weighted = layer_depth_factor.astype(jnp.float32)[:, None, None, None] * smoothed.astype(jnp.float32)
    from_ground = jnp.cumsum(weighted[::-1], axis=0)[::-1]
    geopotential = (from_ground - 0.5 * weighted).astype(jnp.bfloat16)
    grid = jnp.stack([smoothed, geopotential], axis=1).astype(jnp.float32)
    spectrum = jnp.fft.rfft(grid, axis=-1)[..., :K] / math.sqrt(ZONAL_POINTS)
    fourier = jnp.stack([jnp.real(spectrum), jnp.imag(spectrum)], axis=2).astype(jnp.bfloat16)
    half_k = K // 2
    channels = VERTICAL_LAYERS * 4
    north = fourier[:, :, :, 0].reshape(channels, half_rows, K)
    south = fourier[:, :, :, 1].reshape(channels, half_rows, K)
    stacked = jnp.stack([north[..., :half_k], south[..., :half_k], north[..., ::-1][..., :half_k], south[..., ::-1][..., :half_k]], axis=0)
    arranged = jnp.transpose(stacked, (3, 0, 1, 2)).reshape(half_k, 4 * channels, half_rows).astype(jnp.float32)

    def pair_block(block_start):
        coeff_block = lax.dynamic_slice_in_dim(arranged, block_start, 32, 0)
        table_block = lax.dynamic_slice_in_dim(weighted_polynomial_table, block_start, 32, 1).astype(jnp.float32)
        products = jnp.einsum('pkj,jpq->pkq', coeff_block, table_block)
        return pair_terms(products, block_start + jnp.arange(32, dtype=jnp.int32), K + 1)
    starts = jnp.arange(0, half_k, 32, dtype=jnp.int32)
    by_pair = lax.map(pair_block, starts).reshape(half_k, channels, K + 1)
    by_slot = jnp.take(by_pair, wavenumber_to_mode_degree.astype(jnp.int32), axis=0)
    spectral = jnp.transpose(by_slot.reshape(half_k, VERTICAL_LAYERS, 2, 2, K + 1), (1, 2, 3, 0, 4))
    return (smoothed, spectral)
```

```python
import math

import jax
import jax.numpy as jnp
import ml_dtypes
import numpy as np
from jax import lax
from jax.experimental import pallas as pl
from jax.experimental.pallas import tpu as pltpu
from jax.sharding import PartitionSpec as P

LON = 4096
HALF = LON // 2
STEPS = 1024
K = 640
HK = K // 2
ROWS = 8
NZ = 16
SLOTS = 5
F32 = jnp.float32
BF16 = jnp.bfloat16
CHUNKS = (
    ((0, 0), (1, 0), (0, 1), (1, 1), (0, 2), (1, 2)),
    ((0, 3), (1, 3), (0, 4), (1, 4), (None, 5)),
)
ZROWS = 32
TILES = sum(len(c) for c in CHUNKS)
ZORDER = (8, 7, 9, 6, 10, 5, 11, 4, 12, 3, 13, 2, 14, 1, 15)


def fourier_table():
    p = np.arange(HK)
    m = np.concatenate([p, K - 1 - p])
    phase = (m[:, None] * np.arange(HALF)[None, :]) % LON
    angle = phase * (2.0 * math.pi / LON)
    table = np.concatenate([np.cos(angle), -np.sin(angle)], axis=0) / math.sqrt(LON)
    return table.astype(ml_dtypes.bfloat16)


def spread_tables():
    out = np.zeros((4, 2, 2, ROWS, ROWS, 128), np.float32)
    lane = np.arange(128)
    for half in range(2):
        for hem in range(2):
            a = np.ones(128) if hem == 0 else 1.0 - 2.0 * (lane % 2)
            b = np.ones(128) if hem == 0 else 1.0 - 2.0 * ((lane + 1 - half) % 2)
            for j in range(ROWS):
                out[0, half, hem, j, j] = a
                out[1, half, hem, j, j] = b
                out[2, half, hem, j, j, 0] = b[0]
                out[3, half, hem, j, j, 1] = b[0]
    return out.reshape(4 * 4 * ROWS, ROWS * 128).astype(ml_dtypes.bfloat16)


def nt(a, b):
    return lax.dot_general(a, b, (((1,), (1,)), ((), ())), preferred_element_type=F32)


def kernel(
    air, kappa, before, after, thick, perm, w_hbm, e_hbm, t_hbm,
    smooth, spectral,
    w, e, t, x, onehot, coef_a, coef_b, coef_x, partial,
    core_send, core_recv, own, x_send, x_recv, summed, packed, z_send, z_recv,
    field, lev_send, lev_recv,
    in_sem, core_sem, x_sem, zs_sem, zr_sem, ls_sem, lr_sem,
):
    band = lax.axis_index("band")
    lev = lax.axis_index("lev")
    z, xlo, core = band // 4, (band // 2) % 2, band % 2

    def at(zz, xx, cc, ll):
        return ((zz * 2 + xx) * 2 + cc, ll)

    core_peer = at(z, xlo, 1 - core, lev)
    x_peer = at(z, 1 - xlo, core, lev)
    z_peer = {d: at((z + d) % NZ, xlo, core, lev) for d in range(1, NZ)}
    lev_peer = {d: at(z, xlo, core, (lev + 8 - d) % 8) for d in range(1, 8)}
    mesh_id = pl.DeviceIdType.MESH

    barrier = pltpu.get_barrier_semaphore()
    peers = [core_peer, x_peer, *z_peer.values(), *lev_peer.values()]
    for peer in peers:
        pl.semaphore_signal(barrier, inc=1, device_id=peer, device_id_type=mesh_id)

    loads = [
        pltpu.make_async_copy(
            w_hbm.at[pl.ds(k * HK, HK)], w.at[pl.ds(k * HK, HK)], in_sem.at[k]
        )
        for k in range(4)
    ]
    loads.append(pltpu.make_async_copy(e_hbm, e, in_sem.at[4]))
    loads.append(pltpu.make_async_copy(t_hbm, t, in_sem.at[5]))
    for load in loads:
        load.start()

    row = lax.broadcasted_iota(jnp.int32, (ROWS, 1), 0)
    j = (band * ROWS + row).astype(F32)
    step = math.pi / STEPS
    centre = jnp.sin((j + 0.5) * step)
    upper = jnp.sin((j + 1.0) * step) / centre
    lower = jnp.sin(j * step) / centre
    last = band == 63
    folded = []
    for hem in range(2):
        u = air[0, hem].astype(F32)
        kap = kappa[hem].astype(F32)
        pole = before[hem : hem + 1, :].astype(F32)
        across = air[0, 1 - hem].astype(F32)[ROWS - 1 :, :]
        beyond = jnp.where(last, across, after[hem : hem + 1, :].astype(F32))
        prev = jnp.where(row == 0, pole, pltpu.roll(u, 1, 0))
        succ = jnp.where(row == ROWS - 1, beyond, pltpu.roll(u, ROWS - 1, 0))
        east = pltpu.roll(u, LON - 1, 1)
        west = pltpu.roll(u, 1, 1)
        s = u + kap * (east - 2.0 * u + west + upper * (succ - u) - lower * (u - prev))
        s = s.astype(BF16)
        smooth[0, hem] = s
        s = s.astype(F32)
        folded.append((s[:, :HALF] + s[:, HALF:], s[:, :HALF] - s[:, HALF:]))
    for half in range(2):
        x[pl.ds(16 * half, 16), :] = jnp.concatenate(
            [folded[0][half], folded[1][half]], axis=0
        ).astype(BF16)

    r = lax.broadcasted_iota(jnp.int32, (HK, HK), 0)
    col = lax.broadcasted_iota(jnp.int32, (HK, HK), 1)
    group = (r * 205) >> 10
    dz, dx, dc = group & 15, (group >> 4) & 1, group >> 5
    to_x = jnp.where(dx == 0, 1 - xlo, xlo)
    to_c = jnp.where(dc == 0, 1 - core, core)
    slot = ((((z + dz) & 15) * 2 + to_x) * 2 + to_c) * SLOTS + (r - 5 * group)
    order = jnp.where(slot == col, 1.0, 0.0).astype(BF16)
    pair_of = jnp.where(r == perm[...], 1.0, 0.0).astype(BF16)
    onehot[...] = nt(order, pair_of).astype(BF16)

    pairs = lax.broadcasted_iota(jnp.int32, (HK, 32), 0)
    lanes = lax.broadcasted_iota(jnp.int32, (HK, 32), 1)
    loads[4].wait()
    xs = x[...]
    for k in range(4):
        loads[k].wait()
        sums = nt(w[pl.ds(k * HK, HK), :], xs)
        part, back = k // 2, k % 2
        keep = (lanes < 16) == ((pairs + back) % 2 == 0)
        f = jnp.where(keep, sums, 0.0).astype(BF16)
        target = coef_b if back else coef_a
        target[part] = jnp.dot(
            f, e[pl.ds(32 * back, 32), :], preferred_element_type=F32
        )
        if back:
            c = jnp.dot(
                f, e[pl.ds(64 + 32 * part, 32), :], preferred_element_type=F32
            )
            if part == 0:
                coef_x[...] = c
            else:
                coef_x[...] += c
    loads[5].wait()

    def legendre(q, first, count, kind):
        lane = lax.broadcasted_iota(jnp.int32, (16, 128), 1)
        sub = lax.broadcasted_iota(jnp.int32, (16, 128), 0)

        def body(i, carry):
            p0 = pl.multiple_of((first + i) * 16, 16)
            acc = [jnp.zeros((16, 128), F32) for _ in range(2)]
            if kind == "ab":
                front = 128 * q + lane < K - p0 - sub
            for jj in range(ROWS):
                tt = t[jj, pl.ds(p0, 16), 128 * q : 128 * q + 128].astype(F32)
                for part in range(2):
                    where = (part, pl.ds(p0, 16), pl.ds(128 * jj, 128))
                    if kind == "a":
                        c = coef_a[where]
                    elif kind == "b":
                        c = coef_b[where]
                    else:
                        c = jnp.where(front, coef_a[where], coef_b[where])
                    acc[part] = acc[part] + c * tt
            for part in range(2):
                place = 128 * (2 * q + part)
                partial[pl.ds(p0, 16), place : place + 128] = acc[part].astype(BF16)
            return carry

        lax.fori_loop(0, count, body, 0)

    def legendre_last():
        def body(i, carry):
            p0 = pl.multiple_of(i * 16, 16)
            acc = jnp.zeros((16, 128), F32)
            for jj in range(ROWS):
                tt = t[jj, pl.ds(p0, 16), K : K + 1].astype(F32)
                acc = acc + coef_x[pl.ds(p0, 16), pl.ds(128 * jj, 128)] * tt
            partial[pl.ds(p0, 16), 10 * 128 :] = acc.astype(BF16)
            return carry

        lax.fori_loop(0, HK // 16, body, 0)

    def sums_of(q):
        full = min(max((K - 127 - 128 * q) // 16, 0), HK // 16)
        none = min((K - 128 * q) // 16, HK // 16)
        for lo, hi, kind in (
            (0, full, "a"),
            (full, none, "ab"),
            (none, HK // 16, "b"),
        ):
            if hi > lo:
                legendre(q, lo, hi - lo, kind)

    core_copy, x_copy, z_copy = {}, {}, {}
    offset = (0, 128 * len(CHUNKS[0]))

    def core_step(c):
        n = 128 * len(CHUNKS[c])
        cols = slice(offset[c], offset[c] + n)
        mine = partial[:, cols]
        core_send[:, cols] = jnp.dot(
            onehot[pl.ds(0, 160), :], mine, preferred_element_type=F32
        ).astype(BF16)
        core_copy[c] = pltpu.make_async_remote_copy(
            src_ref=core_send.at[:, cols],
            dst_ref=core_recv.at[:, cols],
            send_sem=core_sem.at[0, c],
            recv_sem=core_sem.at[1, c],
            device_id=core_peer,
            device_id_type=mesh_id,
        )
        if c == 0:
            pl.semaphore_wait(barrier, len(peers))
        core_copy[c].start()
        own[:, cols] = jnp.dot(
            onehot[pl.ds(160, 160), :], mine, preferred_element_type=F32
        )

    def x_step(c):
        n = 128 * len(CHUNKS[c])
        cols = slice(offset[c], offset[c] + n)
        core_copy[c].wait_recv()
        x_send[:, cols] = (
            own[pl.ds(0, 80), cols] + core_recv[pl.ds(0, 80), cols].astype(F32)
        ).astype(BF16)
        x_copy[c] = pltpu.make_async_remote_copy(
            src_ref=x_send.at[:, cols],
            dst_ref=x_recv.at[:, cols],
            send_sem=x_sem.at[0, c],
            recv_sem=x_sem.at[1, c],
            device_id=x_peer,
            device_id_type=mesh_id,
        )
        x_copy[c].start()

    def z_step(c):
        n = 128 * len(CHUNKS[c])
        cols = slice(offset[c], offset[c] + n)
        x_copy[c].wait_recv()
        summed[:, cols] = (
            own[pl.ds(80, 80), cols]
            + core_recv[pl.ds(80, 80), cols].astype(F32)
            + x_recv[:, cols].astype(F32)
        )
        for d in range(NZ):
            for i in range(len(CHUNKS[c])):
                packed[c, d, 5 * i : 5 * i + 5, :] = summed[
                    5 * d : 5 * d + 5, offset[c] + 128 * i : offset[c] + 128 * i + 128
                ]
        for d in range(1, NZ):
            z_send[c, d] = packed[c, d].astype(BF16)
        z_copy[c] = []
        for d in ZORDER:
            copy = pltpu.make_async_remote_copy(
                src_ref=z_send.at[c, d],
                dst_ref=z_recv.at[c, d],
                send_sem=zs_sem.at[c, d],
                recv_sem=zr_sem.at[c, d],
                device_id=z_peer[d],
                device_id_type=mesh_id,
            )
            copy.start()
            z_copy[c].append(copy)

    packed[...] = jnp.zeros_like(packed)
    sums_of(0)
    sums_of(1)
    sums_of(2)
    core_step(0)
    sums_of(3)
    x_step(0)
    sums_of(4)
    legendre_last()
    core_step(1)
    x_step(1)
    z_step(0)
    z_step(1)

    thickness = thick[0]
    for c in range(len(CHUNKS)):
        for copy in z_copy[c]:
            copy.wait_recv()
        total = packed[c, 0]
        for d in range(1, NZ):
            total = total + z_recv[c, d].astype(F32)
        field[0, pl.ds(ZROWS * c, ZROWS), :] = total
        lev_send[pl.ds(ZROWS * c, ZROWS), :] = (total * thickness).astype(BF16)
    lev_copy = {
        d: pltpu.make_async_remote_copy(
            src_ref=lev_send,
            dst_ref=lev_recv.at[d],
            send_sem=ls_sem.at[d],
            recv_sem=lr_sem.at[d],
            device_id=lev_peer[d],
            device_id_type=mesh_id,
        )
        for d in range(1, 8)
    }
    for d in range(7, 0, -1):

        @pl.when(lev >= d)
        def _():
            lev_copy[d].start()

    field[1] = (0.5 * thickness) * field[0]

    def put(f):
        for c, tiles in enumerate(CHUNKS):
            for n, (part, q) in enumerate(tiles):
                for i in range(SLOTS):
                    k = ZROWS * c + 5 * n + i
                    if part is None:
                        for half in range(2):
                            spectral[f, i, half : half + 1, K : K + 1] = field[
                                f, k : k + 1, half : half + 1
                            ]
                    else:
                        spectral[f, i, part : part + 1, 128 * q : 128 * q + 128] = (
                            field[f, k : k + 1, :]
                        )

    put(0)
    for d in range(1, 8):

        @pl.when(lev + d < 8)
        def _():
            lev_copy[d].wait_recv()
            field[1] += lev_recv[d].astype(F32)

    put(1)

    for c in range(len(CHUNKS)):
        core_copy[c].wait_send()
        x_copy[c].wait_send()
        for copy in z_copy[c]:
            copy.wait_send()
    for d in range(1, 8):

        @pl.when(lev >= d)
        def _():
            lev_copy[d].wait_send()


def on_device(air, kappa, thick, table, perm):
    tail = air[0, :, ROWS - 1, :]
    head = air[0, :, 0, :]
    before = lax.ppermute(tail, "band", [(i, i + 1) for i in range(63)])
    after = lax.ppermute(head, "band", [(i + 1, i) for i in range(63)])
    vmem = pl.BlockSpec(memory_space=pltpu.VMEM)
    hbm = pl.BlockSpec(memory_space=pl.ANY)
    nc = len(CHUNKS)
    wide = 128 * TILES
    smooth, spectral = pl.pallas_call(
        kernel,
        out_shape=(
            jax.ShapeDtypeStruct((1, 2, ROWS, LON), BF16),
            jax.ShapeDtypeStruct((2, SLOTS, 2, K + 1), F32),
        ),
        in_specs=[
            vmem, vmem, vmem, vmem, pl.BlockSpec(memory_space=pltpu.SMEM), vmem,
            hbm, hbm, hbm,
        ],
        out_specs=(vmem, vmem),
        scratch_shapes=[
            pltpu.VMEM((4 * HK, HALF), BF16),
            pltpu.VMEM((128, ROWS * 128), BF16),
            pltpu.VMEM((ROWS, HK, K + 1), BF16),
            pltpu.VMEM((32, HALF), BF16),
            pltpu.VMEM((HK, HK), BF16),
            pltpu.VMEM((2, HK, ROWS * 128), F32),
            pltpu.VMEM((2, HK, ROWS * 128), F32),
            pltpu.VMEM((HK, ROWS * 128), F32),
            pltpu.VMEM((HK, wide), BF16),
            pltpu.VMEM((160, wide), BF16),
            pltpu.VMEM((160, wide), BF16),
            pltpu.VMEM((160, wide), F32),
            pltpu.VMEM((80, wide), BF16),
            pltpu.VMEM((80, wide), BF16),
            pltpu.VMEM((80, wide), F32),
            pltpu.VMEM((nc, NZ, ZROWS, 128), F32),
            pltpu.VMEM((nc, NZ, ZROWS, 128), BF16),
            pltpu.VMEM((nc, NZ, ZROWS, 128), BF16),
            pltpu.VMEM((2, nc * ZROWS, 128), F32),
            pltpu.VMEM((nc * ZROWS, 128), BF16),
            pltpu.VMEM((8, nc * ZROWS, 128), BF16),
            pltpu.SemaphoreType.DMA((6,)),
            pltpu.SemaphoreType.DMA((2, nc)),
            pltpu.SemaphoreType.DMA((2, nc)),
            pltpu.SemaphoreType.DMA((nc, NZ)),
            pltpu.SemaphoreType.DMA((nc, NZ)),
            pltpu.SemaphoreType.DMA((8,)),
            pltpu.SemaphoreType.DMA((8,)),
        ],
        compiler_params=pltpu.CompilerParams(
            collective_id=0, has_side_effects=True, vmem_limit_bytes=56 * 2**20
        ),
        name="transform",
    )(
        air,
        kappa,
        before,
        after,
        thick,
        perm.reshape(1, HK),
        jnp.asarray(fourier_table()),
        jnp.asarray(spread_tables()),
        table,
    )
    return smooth, jnp.transpose(spectral, (0, 2, 1, 3))[None]


def solution(mesh):
    return jax.shard_map(
        on_device,
        mesh=mesh,
        in_specs=(
            P("lev", None, "band", None),
            P(None, "band", None),
            P("lev"),
            P("band", None, None),
            P(),
        ),
        out_specs=(P("lev", None, "band", None), P("lev", None, None, "band", None)),
        check_vma=False,
    )
```

```python
import math

import jax
import jax.numpy as jnp
import ml_dtypes
import numpy as np
from jax import lax
from jax.experimental import pallas as pl
from jax.experimental.pallas import tpu as pltpu
from jax.sharding import PartitionSpec as P

LON = 4096
FOLD = 4
WAVE = LON // FOLD
STEPS = 1024
K = 640
HK = K // 2
ROWS = 8
NZ = 16
SLOTS = 5
F32 = jnp.float32
BF16 = jnp.bfloat16
CHUNKS = (
    ((0, 0), (1, 0), (0, 1)),
    ((1, 1), (0, 2), (1, 2)),
    ((0, 3), (1, 3)),
    ((0, 4), (1, 4), (None, 5)),
)
PLACE = {tile: k for k, tile in enumerate(t for c in CHUNKS for t in c)}
START = tuple(128 * PLACE[c[0]] for c in CHUNKS)
ZROWS = 16
TILES = len(PLACE)
LAST = (0, 2)
ZORDER = (8, 7, 9, 6, 10, 5, 11, 4, 12, 3, 13, 2, 14, 1, 15)


def fourier_table():
    p = np.arange(HK)
    m = np.concatenate([p, K - 1 - p])
    angle = (m[:, None] * np.arange(WAVE)[None, :] % LON) * (2.0 * math.pi / LON)
    table = np.concatenate([np.cos(angle), -np.sin(angle)], axis=0) / math.sqrt(LON)
    return table.astype(ml_dtypes.bfloat16)


def spread_tables():
    out = np.zeros((2, 4, 2, ROWS, ROWS, 128), np.float32)
    lane = np.arange(128)
    for group in range(4):
        odd_pair = 1 if group < 2 else 0
        for j in range(ROWS):
            out[:, group, 0, j, j] = 1.0
            out[0, group, 1, j, j] = 1.0 - 2.0 * (lane % 2)
            out[1, group, 1, j, j] = 1.0 - 2.0 * ((lane + odd_pair) % 2)
    return out.reshape(2 * 8 * ROWS, ROWS * 128).astype(ml_dtypes.bfloat16)


def nt(a, b):
    return lax.dot_general(a, b, (((1,), (1,)), ((), ())), preferred_element_type=F32)


def kernel(
    air_hbm, kappa_hbm, thick, perm_hbm, w_hbm, e_hbm, t_hbm,
    smooth_hbm, field,
    air, kappa, perm, smooth,
    halo_rows, halo_send, halo_recv, base, x_base, w, e, t, xc, xs, onehot, coef_a, coef_b, partial,
    core_send, core_recv, own, x_send, x_recv, summed, packed, z_send, z_recv,
    lev_send, lev_recv,
    in_sem, out_sem, halo_sem, core_sem, x_sem, zs_sem, zr_sem, ls_sem, lr_sem, told,
):
    band = lax.axis_index("band")
    lev = lax.axis_index("lev")
    z, xlo, core = band // 4, (band // 2) % 2, band % 2

    def at(zz, xx, cc, ll):
        return ((zz * 2 + xx) * 2 + cc, ll)

    yy, xhi = lev // 2, lev % 2
    core_peer = at(z, xlo, 1 - core, lev)
    x_peer = at(z, 1 - xlo, core, lev)
    z_peer = {d: at((z + d) % NZ, xlo, core, lev) for d in range(1, NZ)}
    lev_peer = {d: at(z, xlo, core, (lev + 8 - d) % 8) for d in range(1, 8)}
    y_peer = {d: at(z, xlo, core, ((yy + d) % 4) * 2 + xhi) for d in (1, 3)}
    far_x_peer = at(z, xlo, core, yy * 2 + 1 - xhi)
    halo_peer = (((band + 1) % 64, lev), ((band + 63) % 64, lev))
    mesh_id = pl.DeviceIdType.MESH

    barrier = pltpu.get_barrier_semaphore()
    peers = [
        *halo_peer, x_peer, z_peer[1], z_peer[15], y_peer[1], y_peer[3], far_x_peer,
    ]
    for peer in peers:
        pl.semaphore_signal(barrier, inc=1, device_id=peer, device_id_type=mesh_id)

    def tell(k, peer):
        pl.semaphore_signal(
            told.at[k], inc=1, device_id=peer, device_id_type=mesh_id
        )

    def heard(*ks):
        for k in ks:
            pl.semaphore_wait(told.at[k], 1)

    loads = [
        pltpu.make_async_copy(src, dst, in_sem.at[n])
        for n, (src, dst) in enumerate(
            [(air_hbm, air), (kappa_hbm, kappa), (perm_hbm, perm)]
            + [
                (w_hbm.at[pl.ds(k * HK, HK)], w.at[pl.ds(k * HK, HK)])
                for k in (0, 2, 1, 3)
            ]
            + [(e_hbm, e)]
            + [(t_hbm.at[k], t.at[k]) for k in range(ROWS)]
        )
    ]
    for load in loads:
        load.start()
    packed[...] = jnp.zeros_like(packed)

    row = lax.broadcasted_iota(jnp.int32, (ROWS, 1), 0)
    loads[0].wait()
    for hem in range(2):
        base[hem] = air[0, hem].astype(F32)
    for way, r in enumerate((ROWS - 1, 0)):
        for hem in range(2):
            for k in range(8):
                halo_rows[way, 8 * hem + k : 8 * hem + k + 1, :] = base[
                    hem, r : r + 1, 512 * k : 512 * k + 512
                ]
        halo_send[way] = halo_rows[way].astype(BF16)
    pl.semaphore_wait(barrier, len(peers))
    halo_copy = [
        pltpu.make_async_remote_copy(
            src_ref=halo_send.at[way],
            dst_ref=halo_recv.at[way],
            send_sem=halo_sem.at[0, way],
            recv_sem=halo_sem.at[1, way],
            device_id=halo_peer[way],
            device_id_type=mesh_id,
        )
        for way in range(2)
    ]
    for copy in halo_copy:
        copy.start()
    tell(0, z_peer[1])
    tell(1, z_peer[15])
    tell(6, y_peer[1])
    tell(7, y_peer[3])
    j = (band * ROWS + row).astype(F32)
    step = math.pi / STEPS
    centre = jnp.sin((j + 0.5) * step)
    upper = jnp.sin((j + 1.0) * step) / centre
    lower = jnp.sin(j * step) / centre
    last = band == 63
    loads[1].wait()
    for hem in range(2):
        u = base[hem]
        across = base[1 - hem][ROWS - 1 :, :]
        prev = jnp.where(row == 0, 0.0, pltpu.roll(u, 1, 0))
        succ = jnp.where(
            row == ROWS - 1, jnp.where(last, across, 0.0), pltpu.roll(u, ROWS - 1, 0)
        )
        east = pltpu.roll(u, LON - 1, 1)
        west = pltpu.roll(u, 1, 1)
        merid = upper * (succ - u) - lower * (u - prev)
        x_base[hem] = u + kappa[hem].astype(F32) * (east - 2.0 * u + west + merid)

    loads[2].wait()
    r = lax.broadcasted_iota(jnp.int32, (HK, HK), 0)
    col = lax.broadcasted_iota(jnp.int32, (HK, HK), 1)
    group = (r * 205) >> 10
    dz, dx, dc = group & 15, (group >> 4) & 1, group >> 5
    to_x = jnp.where(dx == 0, 1 - xlo, xlo)
    to_c = jnp.where(dc == 0, 1 - core, core)
    slot = ((((z + dz) & 15) * 2 + to_x) * 2 + to_c) * SLOTS + (r - 5 * group)
    order = jnp.where(slot == col, 1.0, 0.0).astype(BF16)
    pair_of = jnp.where(r == perm[...].reshape(1, HK), 1.0, 0.0).astype(BF16)
    onehot[...] = nt(order, pair_of).astype(BF16)

    heard(0, 1, 6, 7)
    tell(2, z_peer[2])
    tell(3, z_peer[14])
    tell(8, far_x_peer)

    folded = []
    for way in range(2):
        halo_copy[way].wait_recv()
        halo_rows[way] = halo_recv[way].astype(F32)
    for hem in range(2):
        pole, beyond = (
            jnp.concatenate(
                [halo_rows[way, 8 * hem + k : 8 * hem + k + 1, :] for k in range(8)],
                axis=1,
            )
            for way in range(2)
        )
        at_pole = jnp.where((row == 0) & (band > 0), lower, 0.0)
        at_edge = jnp.where((row == ROWS - 1) & (band < 63), upper, 0.0)
        s = x_base[hem] + kappa[hem].astype(F32) * (at_pole * pole + at_edge * beyond)
        s = s.astype(BF16)
        smooth[0, hem] = s
        folded.append(s.astype(F32))
    save = pltpu.make_async_copy(smooth, smooth_hbm, out_sem)
    save.start()
    q0, q1, q2, q3 = (
        jnp.concatenate([s[:, WAVE * k : WAVE * k + WAVE] for s in folded], axis=0)
        for k in range(FOLD)
    )
    even, odd = q0 + q2, q1 + q3
    y0, y2 = (even + odd).astype(BF16), (even - odd).astype(BF16)
    d02, d13 = (q0 - q2).astype(BF16), (q1 - q3).astype(BF16)
    for k, (c, d) in enumerate(((y0, y0), (y2, y2), (d02, d13), (d13, d02))):
        xc[pl.ds(16 * k, 16), :] = c
        xs[pl.ds(16 * k, 16), :] = d

    pairs = lax.broadcasted_iota(jnp.int32, (HK, 64), 0)
    group = lax.broadcasted_iota(jnp.int32, (HK, 64), 1) >> 4
    loads[7].wait()
    for back in range(2):
        m = (K - 1 - pairs if back else pairs) & 3
        loads[3 + 2 * back].wait()
        loads[4 + 2 * back].wait()
        cosine = nt(w[pl.ds(back * HK, HK), :], xc[...])
        sine = nt(w[pl.ds(K + back * HK, HK), :], xs[...])
        target = coef_b if back else coef_a
        turn = jnp.where(m == 1, 1.0, -1.0)
        real = cosine + jnp.where(group == 2, turn * sine, 0.0)
        imag = sine - jnp.where(group == 3, turn * cosine, 0.0)
        odd = (m & 1) == 1
        for part, (f, g) in enumerate(((real, 2), (imag, 3))):
            keep = group == jnp.where(odd, g, m >> 1)
            target[part] = jnp.dot(
                jnp.where(keep, f, 0.0).astype(BF16),
                e[pl.ds(64 * back, 64), :],
                preferred_element_type=F32,
            )
    heard(2, 3, 8)
    tell(4, z_peer[4])
    tell(5, z_peer[12])
    for load in loads[8:]:
        load.wait()

    def kind_of(q, block):
        if q == 5:
            return "x"
        if 16 * block + 15 < K - 127 - 128 * q:
            return "a"
        return "b" if 16 * block >= K - 128 * q else "ab"

    def legendre(qs, first, count):
        kinds = [kind_of(q, first) for q in qs]
        lane = lax.broadcasted_iota(jnp.int32, (16, 128), 1)
        sub = lax.broadcasted_iota(jnp.int32, (16, 128), 0)

        def block(p0):
            rows = pl.ds(p0, 16)
            acc = [[jnp.zeros((16, 128), F32) for _ in range(2)] for _ in qs]
            front = [128 * q + lane < K - p0 - sub for q in qs]
            for jj in range(ROWS):
                cols = pl.ds(128 * jj, 128)
                ca = cb = None
                if "a" in kinds or "ab" in kinds:
                    ca = [coef_a[part, rows, cols] for part in range(2)]
                if "b" in kinds or "ab" in kinds or "x" in kinds:
                    cb = [coef_b[part, rows, cols] for part in range(2)]
                for n, (q, kind) in enumerate(zip(qs, kinds)):
                    if kind == "x":
                        tt = t[jj, rows, K : K + 1].astype(F32)
                    else:
                        tt = t[jj, rows, 128 * q : 128 * q + 128].astype(F32)
                    for part in range(2):
                        if kind == "a":
                            c = ca[part]
                        elif kind == "ab":
                            c = jnp.where(front[n], ca[part], cb[part])
                        else:
                            c = cb[part]
                        acc[n][part] = acc[n][part] + c * tt
            for n, (q, kind) in enumerate(zip(qs, kinds)):
                if kind == "x":
                    both = jnp.where(lane < LAST[1], acc[n][0], acc[n][1])
                    place = 128 * PLACE[None, q]
                    partial[rows, place : place + 128] = both.astype(BF16)
                else:
                    for part in range(2):
                        place = 128 * PLACE[part, q]
                        partial[rows, place : place + 128] = acc[n][part].astype(BF16)

        def body(i, carry):
            for n in range(2):
                block(pl.multiple_of((first + 2 * i + n) * 16, 16))
            return carry

        lax.fori_loop(0, count // 2, body, 0)

    def sums_of(*qs):
        first = 0
        for block in range(1, HK // 16 + 1):
            if block == HK // 16 or any(
                kind_of(q, block) != kind_of(q, first) for q in qs
            ):
                legendre(qs, first, block - first)
                first = block

    core_copy, x_copy, z_copy = {}, {}, {}
    offset = START

    def core_step(c):
        n = 128 * len(CHUNKS[c])
        cols = slice(offset[c], offset[c] + n)
        mine = partial[:, cols]
        core_send[:, cols] = jnp.dot(
            onehot[pl.ds(0, 160), :], mine, preferred_element_type=F32
        ).astype(BF16)
        core_copy[c] = pltpu.make_async_remote_copy(
            src_ref=core_send.at[:, cols],
            dst_ref=core_recv.at[:, cols],
            send_sem=core_sem.at[0, c],
            recv_sem=core_sem.at[1, c],
            device_id=core_peer,
            device_id_type=mesh_id,
        )
        core_copy[c].start()
        own[:, cols] = jnp.dot(
            onehot[pl.ds(160, 160), :], mine, preferred_element_type=F32
        )

    def x_step(c):
        n = 128 * len(CHUNKS[c])
        cols = slice(offset[c], offset[c] + n)
        core_copy[c].wait_recv()
        x_send[:, cols] = (
            own[pl.ds(0, 80), cols] + core_recv[pl.ds(0, 80), cols].astype(F32)
        ).astype(BF16)
        x_copy[c] = pltpu.make_async_remote_copy(
            src_ref=x_send.at[:, cols],
            dst_ref=x_recv.at[:, cols],
            send_sem=x_sem.at[0, c],
            recv_sem=x_sem.at[1, c],
            device_id=x_peer,
            device_id_type=mesh_id,
        )
        x_copy[c].start()

    def z_step(c):
        n = 128 * len(CHUNKS[c])
        cols = slice(offset[c], offset[c] + n)
        x_copy[c].wait_recv()
        summed[:, cols] = (
            own[pl.ds(80, 80), cols]
            + core_recv[pl.ds(80, 80), cols].astype(F32)
            + x_recv[:, cols].astype(F32)
        )
        for d in range(NZ):
            for i in range(len(CHUNKS[c])):
                packed[c, d, 5 * i : 5 * i + 5, :] = summed[
                    5 * d : 5 * d + 5, offset[c] + 128 * i : offset[c] + 128 * i + 128
                ]
        for d in range(1, NZ):
            z_send[c, d] = packed[c, d].astype(BF16)
        if c == 0:
            heard(4, 5)
        z_copy[c] = []
        for d in ZORDER:
            copy = pltpu.make_async_remote_copy(
                src_ref=z_send.at[c, d],
                dst_ref=z_recv.at[c, d],
                send_sem=zs_sem.at[c, d],
                recv_sem=zr_sem.at[c, d],
                device_id=z_peer[d],
                device_id_type=mesh_id,
            )
            copy.start()
            z_copy[c].append(copy)

    sums_of(0, 1)
    core_step(0)
    sums_of(2)
    core_step(1)
    x_step(0)
    sums_of(3)
    core_step(2)
    x_step(1)
    sums_of(4, 5)
    core_step(3)
    x_step(2)
    z_step(0)
    x_step(3)
    z_step(1)
    z_step(2)
    z_step(3)

    thickness = thick[0]
    for copy in halo_copy:
        copy.wait_send()
    for c in range(len(CHUNKS)):
        for copy in z_copy[c]:
            copy.wait_recv()
        total = packed[c, 0]
        for d in range(1, NZ):
            total = total + z_recv[c, d].astype(F32)
        field[0, pl.ds(ZROWS * c, ZROWS), :] = total
        lev_send[pl.ds(ZROWS * c, ZROWS), :] = (total * thickness).astype(BF16)
    lev_copy = {
        d: pltpu.make_async_remote_copy(
            src_ref=lev_send,
            dst_ref=lev_recv.at[d],
            send_sem=ls_sem.at[d],
            recv_sem=lr_sem.at[d],
            device_id=lev_peer[d],
            device_id_type=mesh_id,
        )
        for d in range(1, 8)
    }
    for d in range(7, 0, -1):

        @pl.when(lev >= d)
        def _():
            lev_copy[d].start()

    field[1] = (0.5 * thickness) * field[0]
    for d in range(1, 8):

        @pl.when(lev + d < 8)
        def _():
            lev_copy[d].wait_recv()
            field[1] += lev_recv[d].astype(F32)

    save.wait()
    for c in range(len(CHUNKS)):
        core_copy[c].wait_send()
        x_copy[c].wait_send()
        for copy in z_copy[c]:
            copy.wait_send()
    for d in range(1, 8):

        @pl.when(lev >= d)
        def _():
            lev_copy[d].wait_send()


def finish(smooth_in, field, smooth_out, spectral, sem):
    copy = pltpu.make_async_copy(smooth_in, smooth_out, sem)
    copy.start()
    for f in range(2):
        for c, tiles in enumerate(CHUNKS):
            for n, (part, q) in enumerate(tiles):
                for i in range(SLOTS):
                    k = ZROWS * c + 5 * n + i
                    if part is None:
                        for half in range(2):
                            spectral[f, i, half : half + 1, K : K + 1] = field[
                                f, k : k + 1, LAST[half] : LAST[half] + 1
                            ]
                    else:
                        spectral[f, i, part : part + 1, 128 * q : 128 * q + 128] = (
                            field[f, k : k + 1, :]
                        )
    copy.wait()


def on_device(air, kappa, thick, table, perm):
    vmem = pl.BlockSpec(memory_space=pltpu.VMEM)
    hbm = pl.BlockSpec(memory_space=pl.ANY)
    nc = len(CHUNKS)
    wide = 128 * TILES
    grid = jax.ShapeDtypeStruct((1, 2, ROWS, LON), BF16)
    smooth, field = pl.pallas_call(
        kernel,
        out_shape=(grid, jax.ShapeDtypeStruct((2, nc * ZROWS, 128), F32)),
        in_specs=[hbm, hbm, pl.BlockSpec(memory_space=pltpu.SMEM), hbm, hbm, hbm, hbm],
        out_specs=(hbm, vmem),
        scratch_shapes=[
            pltpu.VMEM((1, 2, ROWS, LON), BF16),
            pltpu.VMEM((2, ROWS, LON), BF16),
            pltpu.VMEM((HK,), jnp.int32),
            pltpu.VMEM((1, 2, ROWS, LON), BF16),
            pltpu.VMEM((2, 16, 512), F32),
            pltpu.VMEM((2, 16, 512), BF16),
            pltpu.VMEM((2, 16, 512), BF16),
            pltpu.VMEM((2, ROWS, LON), F32),
            pltpu.VMEM((2, ROWS, LON), F32),
            pltpu.VMEM((4 * HK, WAVE), BF16),
            pltpu.VMEM((128, ROWS * 128), BF16),
            pltpu.VMEM((ROWS, HK, K + 1), BF16),
            pltpu.VMEM((64, WAVE), BF16),
            pltpu.VMEM((64, WAVE), BF16),
            pltpu.VMEM((HK, HK), BF16),
            pltpu.VMEM((2, HK, ROWS * 128), F32),
            pltpu.VMEM((2, HK, ROWS * 128), F32),
            pltpu.VMEM((HK, wide), BF16),
            pltpu.VMEM((160, wide), BF16),
            pltpu.VMEM((160, wide), BF16),
            pltpu.VMEM((160, wide), F32),
            pltpu.VMEM((80, wide), BF16),
            pltpu.VMEM((80, wide), BF16),
            pltpu.VMEM((80, wide), F32),
            pltpu.VMEM((nc, NZ, ZROWS, 128), F32),
            pltpu.VMEM((nc, NZ, ZROWS, 128), BF16),
            pltpu.VMEM((nc, NZ, ZROWS, 128), BF16),
            pltpu.VMEM((nc * ZROWS, 128), BF16),
            pltpu.VMEM((8, nc * ZROWS, 128), BF16),
            pltpu.SemaphoreType.DMA((8 + ROWS,)),
            pltpu.SemaphoreType.DMA,
            pltpu.SemaphoreType.DMA((2, 2)),
            pltpu.SemaphoreType.DMA((2, nc)),
            pltpu.SemaphoreType.DMA((2, nc)),
            pltpu.SemaphoreType.DMA((nc, NZ)),
            pltpu.SemaphoreType.DMA((nc, NZ)),
            pltpu.SemaphoreType.DMA((8,)),
            pltpu.SemaphoreType.DMA((8,)),
            pltpu.SemaphoreType.REGULAR((9,)),
        ],
        compiler_params=pltpu.CompilerParams(
            collective_id=0, has_side_effects=True, vmem_limit_bytes=56 * 2**20
        ),
        name="transform",
    )(
        air,
        kappa,
        thick,
        perm,
        jnp.asarray(fourier_table()),
        jnp.asarray(spread_tables()),
        table,
    )
    smooth, spectral = pl.pallas_call(
        finish,
        out_shape=(grid, jax.ShapeDtypeStruct((2, SLOTS, 2, K + 1), F32)),
        in_specs=[vmem, vmem],
        out_specs=(hbm, vmem),
        scratch_shapes=[pltpu.SemaphoreType.DMA],
        name="finish",
    )(smooth, field)
    return smooth, jnp.transpose(spectral, (0, 2, 1, 3))[None]


def solution(mesh):
    return jax.shard_map(
        on_device,
        mesh=mesh,
        in_specs=(
            P("lev", None, "band", None),
            P(None, "band", None),
            P("lev"),
            P("band", None, None),
            P(),
        ),
        out_specs=(P("lev", None, "band", None), P("lev", None, None, "band", None)),
        check_vma=False,
    )
```

```python
import math

import jax
import jax.numpy as jnp
import ml_dtypes
import numpy as np
from jax import lax
from jax.experimental import pallas as pl
from jax.experimental.pallas import tpu as pltpu
from jax.sharding import PartitionSpec as P

LON = 4096
FOLD = 4
WAVE = LON // FOLD
STEPS = 1024
K = 640
HK = K // 2
ROWS = 8
NZ = 16
SLOTS = 5
F32 = jnp.float32
BF16 = jnp.bfloat16
CHUNKS = (
    ((0, 0), (1, 0), (0, 1)),
    ((1, 1), (0, 2), (1, 2)),
    ((0, 3), (1, 3)),
    ((0, 4), (1, 4), (None, 5)),
)
PLACE = {tile: k for k, tile in enumerate(t for c in CHUNKS for t in c)}
START = tuple(128 * PLACE[c[0]] for c in CHUNKS)
ZROWS = 16
TILES = len(PLACE)
LAST = 1
ZORDER = (4, 3, 5, 2, 6, 1, 7)


def fourier_table():
    p = np.arange(HK)
    m = np.concatenate([p, K - 1 - p])
    angle = (m[:, None] * np.arange(WAVE)[None, :] % LON) * (2.0 * math.pi / LON)
    table = np.concatenate([np.cos(angle), -np.sin(angle)], axis=0) / math.sqrt(LON)
    return table.astype(ml_dtypes.bfloat16)


def spread_tables():
    out = np.zeros((2, 4, 2, ROWS, ROWS, 128), np.float32)
    lane = np.arange(128)
    for group in range(4):
        odd_pair = 1 if group < 2 else 0
        for j in range(ROWS):
            out[:, group, 0, j, j] = 1.0
            out[0, group, 1, j, j] = 1.0 - 2.0 * (lane % 2)
            out[1, group, 1, j, j] = 1.0 - 2.0 * ((lane + odd_pair) % 2)
    return out.reshape(2 * 8 * ROWS, ROWS * 128).astype(ml_dtypes.bfloat16)


def nt(a, b):
    return lax.dot_general(a, b, (((1,), (1,)), ((), ())), preferred_element_type=F32)


def kernel(
    air_hbm, kappa_hbm, thick_hbm, perm_hbm, w_hbm, e_hbm, t_hbm,
    smooth_hbm, field,
    air, kappa, thick, perm, smooth,
    halo_rows, halo_send, halo_recv, base, x_base, w, e, t, xc, xs, onehot, coef, partial,
    core_send, core_recv, own, kept, quad_send, quad_recv, summed, packed, z_send, z_recv,
    lev_send, lev_recv,
    in_sem, out_sem, halo_sem, core_sem, qs_sem, qr_sem, zs_sem, zr_sem, ls_sem, lr_sem, told,
):
    band = lax.axis_index("band")
    lev = lax.axis_index("lev")
    z, xlo, core = band // 4, (band // 2) % 2, band % 2

    def at(zz, xx, cc, ll):
        return ((zz * 2 + xx) * 2 + cc, ll)

    yy, xhi = lev // 2, lev % 2
    core_peer = at(z, xlo, 1 - core, lev)
    pair_z = z + 1 - 2 * (z % 2)
    quad_peer = (
        at(pair_z, 1 - xlo, core, lev),
        at(z, 1 - xlo, core, lev),
        at(pair_z, xlo, core, lev),
    )
    z_peer = {d: at((z + d) % NZ, xlo, core, lev) for d in range(1, NZ)}
    lev_peer = {d: at(z, xlo, core, (lev + 8 - d) % 8) for d in range(1, 8)}
    y_peer = {d: at(z, xlo, core, ((yy + d) % 4) * 2 + xhi) for d in (1, 3)}
    far_x_peer = at(z, xlo, core, yy * 2 + 1 - xhi)
    halo_peer = (((band + 1) % 64, lev), ((band + 63) % 64, lev))
    mesh_id = pl.DeviceIdType.MESH

    barrier = pltpu.get_barrier_semaphore()
    peers = [
        *halo_peer, *quad_peer, z_peer[2], z_peer[14], y_peer[1], y_peer[3], far_x_peer,
    ]
    for peer in peers:
        pl.semaphore_signal(barrier, inc=1, device_id=peer, device_id_type=mesh_id)

    def tell(k, peer):
        pl.semaphore_signal(
            told.at[k], inc=1, device_id=peer, device_id_type=mesh_id
        )

    def heard(*ks):
        for k in ks:
            pl.semaphore_wait(told.at[k], 1)

    loads = [
        pltpu.make_async_copy(src, dst, in_sem.at[n])
        for n, (src, dst) in enumerate(
            [(air_hbm, air), (kappa_hbm, kappa), (perm_hbm, perm)]
            + [
                (w_hbm.at[pl.ds(k * HK, HK)], w.at[pl.ds(k * HK, HK)])
                for k in (0, 2, 1, 3)
            ]
            + [(e_hbm, e)]
            + [(thick_hbm, thick)]
            + [(t_hbm.at[k], t.at[k]) for k in range(ROWS)]
        )
    ]
    for load in loads:
        load.start()
    packed[...] = jnp.zeros_like(packed)

    row = lax.broadcasted_iota(jnp.int32, (ROWS, 1), 0)
    loads[0].wait()
    for hem in range(2):
        base[hem] = air[0, hem].astype(F32)
    for way, r in enumerate((ROWS - 1, 0)):
        for hem in range(2):
            for k in range(8):
                halo_rows[way, 8 * hem + k : 8 * hem + k + 1, :] = base[
                    hem, r : r + 1, 512 * k : 512 * k + 512
                ]
        halo_send[way] = halo_rows[way].astype(BF16)
    pl.semaphore_wait(barrier, len(peers))
    halo_copy = [
        pltpu.make_async_remote_copy(
            src_ref=halo_send.at[way],
            dst_ref=halo_recv.at[way],
            send_sem=halo_sem.at[0, way],
            recv_sem=halo_sem.at[1, way],
            device_id=halo_peer[way],
            device_id_type=mesh_id,
        )
        for way in range(2)
    ]
    for copy in halo_copy:
        copy.start()
    tell(0, z_peer[2])
    tell(1, z_peer[14])
    tell(5, y_peer[1])
    tell(6, y_peer[3])
    j = (band * ROWS + row).astype(F32)
    step = math.pi / STEPS
    centre = jnp.sin((j + 0.5) * step)
    upper = jnp.sin((j + 1.0) * step) / centre
    lower = jnp.sin(j * step) / centre
    last = band == 63
    loads[1].wait()
    for hem in range(2):
        u = base[hem]
        across = base[1 - hem][ROWS - 1 :, :]
        prev = jnp.where(row == 0, 0.0, pltpu.roll(u, 1, 0))
        succ = jnp.where(
            row == ROWS - 1, jnp.where(last, across, 0.0), pltpu.roll(u, ROWS - 1, 0)
        )
        east = pltpu.roll(u, LON - 1, 1)
        west = pltpu.roll(u, 1, 1)
        merid = upper * (succ - u) - lower * (u - prev)
        x_base[hem] = u + kappa[hem].astype(F32) * (east - 2.0 * u + west + merid)

    loads[2].wait()
    r = lax.broadcasted_iota(jnp.int32, (HK, HK), 0)
    col = lax.broadcasted_iota(jnp.int32, (HK, HK), 1)
    group = (r * 205) >> 10
    dz, dp, dx, dc = group & 7, (group >> 3) & 1, (group >> 4) & 1, group >> 5
    to_z = (jnp.where(dp == 0, pair_z, z) + 2 * dz) & 15
    to_x = jnp.where(dx == 0, 1 - xlo, xlo)
    to_c = jnp.where(dc == 0, 1 - core, core)
    slot = ((to_z * 2 + to_x) * 2 + to_c) * SLOTS + (r - 5 * group)
    order = jnp.where(slot == col, 1.0, 0.0).astype(BF16)
    pair_of = jnp.where(r == perm[...].reshape(1, HK), 1.0, 0.0).astype(BF16)
    onehot[...] = nt(order, pair_of).astype(BF16)

    heard(0, 1, 5, 6)
    tell(2, z_peer[4])
    tell(3, z_peer[12])
    tell(4, far_x_peer)

    folded = []
    for way in range(2):
        halo_copy[way].wait_recv()
        halo_rows[way] = halo_recv[way].astype(F32)
    for hem in range(2):
        pole, beyond = (
            jnp.concatenate(
                [halo_rows[way, 8 * hem + k : 8 * hem + k + 1, :] for k in range(8)],
                axis=1,
            )
            for way in range(2)
        )
        at_pole = jnp.where((row == 0) & (band > 0), lower, 0.0)
        at_edge = jnp.where((row == ROWS - 1) & (band < 63), upper, 0.0)
        s = x_base[hem] + kappa[hem].astype(F32) * (at_pole * pole + at_edge * beyond)
        s = s.astype(BF16)
        smooth[0, hem] = s
        folded.append(s.astype(F32))
    save = pltpu.make_async_copy(smooth, smooth_hbm, out_sem)
    save.start()
    q0, q1, q2, q3 = (
        jnp.concatenate([s[:, WAVE * k : WAVE * k + WAVE] for s in folded], axis=0)
        for k in range(FOLD)
    )
    even, odd = q0 + q2, q1 + q3
    y0, y2 = (even + odd).astype(BF16), (even - odd).astype(BF16)
    d02, d13 = (q0 - q2).astype(BF16), (q1 - q3).astype(BF16)
    for k, (c, d) in enumerate(((y0, y0), (y2, y2), (d02, d13), (d13, d02))):
        xc[pl.ds(16 * k, 16), :] = c
        xs[pl.ds(16 * k, 16), :] = d

    pairs = lax.broadcasted_iota(jnp.int32, (HK, 64), 0)
    group = lax.broadcasted_iota(jnp.int32, (HK, 64), 1) >> 4
    loads[7].wait()
    def fourier(back, carry):
        m = jnp.where(back == 1, K - 1 - pairs, pairs) & 3
        for k in range(2):
            pltpu.make_async_copy(
                w_hbm.at[pl.ds(0, HK)], w.at[pl.ds(0, HK)], in_sem.at[3 + 2 * back + k]
            ).wait()
        first = pl.multiple_of(back * HK, HK)
        cosine = nt(w[pl.ds(first, HK), :], xc[...])
        sine = nt(w[pl.ds(K + first, HK), :], xs[...])
        turn = jnp.where(m == 1, 1.0, -1.0)
        real = cosine + jnp.where(group == 2, turn * sine, 0.0)
        imag = sine - jnp.where(group == 3, turn * cosine, 0.0)
        odd = (m & 1) == 1
        for part, (f, g) in enumerate(((real, 2), (imag, 3))):
            keep = group == jnp.where(odd, g, m >> 1)
            coef[back, part] = jnp.dot(
                jnp.where(keep, f, 0.0).astype(BF16),
                e[pl.ds(pl.multiple_of(64 * back, 64), 64), :],
                preferred_element_type=F32,
            )
        return carry

    lax.fori_loop(0, 2, fourier, 0)
    for load in loads[8:]:
        load.wait()

    def kind_of(q, block):
        if q == 5:
            return "x"
        if 16 * block + 15 < K - 127 - 128 * q:
            return "a"
        return "b" if 16 * block >= K - 128 * q else "ab"

    def legendre(qs, first, count):
        kinds = [kind_of(q, first) for q in qs]
        lane = lax.broadcasted_iota(jnp.int32, (16, 128), 1)
        sub = lax.broadcasted_iota(jnp.int32, (16, 128), 0)

        def block(p0):
            rows = pl.ds(p0, 16)
            acc = [[0.0, 0.0] for _ in qs]
            front = [128 * q + lane < K - p0 - sub for q in qs]
            for jj in range(ROWS):
                cols = pl.ds(128 * jj, 128)
                ca = cb = None
                if "a" in kinds or "ab" in kinds:
                    ca = [coef[0, part, rows, cols] for part in range(2)]
                if "b" in kinds or "ab" in kinds or "x" in kinds:
                    cb = [coef[1, part, rows, cols] for part in range(2)]
                for n, (q, kind) in enumerate(zip(qs, kinds)):
                    if kind == "x":
                        tt = t[jj, rows, K : K + 1].astype(F32)
                    else:
                        tt = t[jj, rows, 128 * q : 128 * q + 128].astype(F32)
                    for part in range(2):
                        if kind == "a":
                            c = ca[part]
                        elif kind == "ab":
                            c = jnp.where(front[n], ca[part], cb[part])
                        elif kind == "b":
                            c = cb[part]
                        else:
                            c = cb[part][:, :1]
                        acc[n][part] = acc[n][part] + c * tt
            for n, (q, kind) in enumerate(zip(qs, kinds)):
                if kind == "x":
                    both = jnp.where(lane < LAST, acc[n][0], acc[n][1])
                    place = 128 * PLACE[None, q]
                    partial[rows, place : place + 128] = both.astype(BF16)
                else:
                    for part in range(2):
                        place = 128 * PLACE[part, q]
                        partial[rows, place : place + 128] = acc[n][part].astype(BF16)

        def body(i, carry):
            for n in range(2):
                block(pl.multiple_of((first + 2 * i + n) * 16, 16))
            return carry

        lax.fori_loop(0, count // 2, body, 0)

    def sums_of(*qs):
        first = 0
        for block in range(1, HK // 16 + 1):
            if block == HK // 16 or any(
                kind_of(q, block) != kind_of(q, first) for q in qs
            ):
                legendre(qs, first, block - first)
                first = block

    core_copy, quad_copy, z_copy = {}, {}, {}
    offset = START

    def core_step(c):
        n = 128 * len(CHUNKS[c])
        cols = slice(offset[c], offset[c] + n)
        mine = partial[:, cols]
        core_send[:, cols] = jnp.dot(
            onehot[pl.ds(0, 160), :], mine, preferred_element_type=F32
        ).astype(BF16)
        core_copy[c] = pltpu.make_async_remote_copy(
            src_ref=core_send.at[:, cols],
            dst_ref=core_recv.at[:, cols],
            send_sem=core_sem.at[0, c],
            recv_sem=core_sem.at[1, c],
            device_id=core_peer,
            device_id_type=mesh_id,
        )
        core_copy[c].start()
        own[:, cols] = jnp.dot(
            onehot[pl.ds(160, 160), :], mine, preferred_element_type=F32
        )

    def quad_step(c):
        count = len(CHUNKS[c])
        cols = slice(offset[c], offset[c] + 128 * count)
        core_copy[c].wait_recv()
        both = own[:, cols] + core_recv[:, cols].astype(F32)
        parts = [
            [both[40 * g : 40 * g + 40, 128 * n : 128 * n + 128] for n in range(count)]
            for g in range(4)
        ]
        quad_copy[c] = []
        for g in range(3):
            pad = [] if count == 2 else [jnp.zeros((8, 128), F32)]
            rows = pl.ds(0, 40 * count + 8 * len(pad))
            quad_send[c, g, rows, :] = jnp.concatenate(parts[g] + pad, axis=0).astype(
                BF16
            )
            copy = pltpu.make_async_remote_copy(
                src_ref=quad_send.at[c, g, rows],
                dst_ref=quad_recv.at[c, g, rows],
                send_sem=qs_sem.at[c, g],
                recv_sem=qr_sem.at[c, g],
                device_id=quad_peer[g],
                device_id_type=mesh_id,
            )
            copy.start()
            quad_copy[c].append(copy)
        kept[c, pl.ds(0, 40 * count), :] = jnp.concatenate(parts[3], axis=0)

    def z_step(c):
        count = len(CHUNKS[c])
        rows = 40 * count
        total = kept[c, pl.ds(0, rows), :]
        size = rows + (8 if count == 3 else 0)
        for g in range(3):
            quad_copy[c][g].wait_recv()
            total = total + quad_recv[c, g, pl.ds(0, size), :].astype(F32)[:rows, :]
        summed[c, pl.ds(0, rows), :] = total
        for d in range(NZ // 2):
            for n in range(count):
                packed[c, d, 5 * n : 5 * n + 5, :] = summed[
                    c, 40 * n + 5 * d : 40 * n + 5 * d + 5, :
                ]
        if c == 0:
            heard(2, 3, 4)
        z_copy[c] = []
        for d in ZORDER:
            z_send[c, d] = packed[c, d].astype(BF16)
            copy = pltpu.make_async_remote_copy(
                src_ref=z_send.at[c, d],
                dst_ref=z_recv.at[c, d],
                send_sem=zs_sem.at[c, d],
                recv_sem=zr_sem.at[c, d],
                device_id=z_peer[2 * d],
                device_id_type=mesh_id,
            )
            copy.start()
            z_copy[c].append(copy)

    sums_of(0, 1)
    core_step(0)
    sums_of(2)
    core_step(1)
    quad_step(0)
    sums_of(3)
    core_step(2)
    quad_step(1)
    sums_of(4, 5)
    core_step(3)
    quad_step(2)
    quad_step(3)
    z_step(0)
    z_step(1)
    z_step(2)
    z_step(3)

    thickness = thick[...].reshape(1, 1)
    for copy in halo_copy:
        copy.wait_send()
    half = len(CHUNKS) // 2 * ZROWS
    lev_copy = {}
    for c in range(len(CHUNKS)):
        for copy in z_copy[c]:
            copy.wait_recv()
        total = packed[c, 0]
        for d in range(1, NZ // 2):
            total = total + z_recv[c, d].astype(F32)
        rows = pl.ds(ZROWS * c, ZROWS)
        total_w = total * thickness
        lev_send[rows, :] = total_w.astype(BF16)
        field[0, rows, :] = total
        field[1, rows, :] = 0.5 * total_w
        if c % 2:
            h = c // 2
            part = pl.ds(half * h, half)
            for d in range(7, 0, -1):
                lev_copy[h, d] = pltpu.make_async_remote_copy(
                    src_ref=lev_send.at[part],
                    dst_ref=lev_recv.at[d, part],
                    send_sem=ls_sem.at[h, d],
                    recv_sem=lr_sem.at[h, d],
                    device_id=lev_peer[d],
                    device_id_type=mesh_id,
                )

                @pl.when(lev >= d)
                def _():
                    lev_copy[h, d].start()

    for d in range(1, 8):

        @pl.when(lev + d < 8)
        def _():
            lev_copy[0, d].wait_recv()
            lev_copy[1, d].wait_recv()
            field[1] += lev_recv[d].astype(F32)

    save.wait()
    for c in range(len(CHUNKS)):
        core_copy[c].wait_send()
        for copy in quad_copy[c] + z_copy[c]:
            copy.wait_send()
    for d in range(1, 8):

        @pl.when(lev >= d)
        def _():
            lev_copy[0, d].wait_send()
            lev_copy[1, d].wait_send()


def finish(smooth_in, field, smooth_out, spectral, sem):
    copy = pltpu.make_async_copy(smooth_in, smooth_out, sem)
    copy.start()
    for f in range(2):
        for c, tiles in enumerate(CHUNKS):
            for n, (part, q) in enumerate(tiles):
                for i in range(SLOTS):
                    k = ZROWS * c + 5 * n + i
                    if part is None:
                        for half in range(2):
                            spectral[f, i, half : half + 1, K : K + 1] = field[
                                f, k : k + 1, LAST * half : LAST * half + 1
                            ]
                    else:
                        spectral[f, i, part : part + 1, 128 * q : 128 * q + 128] = (
                            field[f, k : k + 1, :]
                        )
    copy.wait()


def on_device(air, kappa, thick, table, perm):
    vmem = pl.BlockSpec(memory_space=pltpu.VMEM)
    hbm = pl.BlockSpec(memory_space=pl.ANY)
    nc = len(CHUNKS)
    wide = 128 * TILES
    grid = jax.ShapeDtypeStruct((1, 2, ROWS, LON), BF16)
    smooth, field = pl.pallas_call(
        kernel,
        out_shape=(grid, jax.ShapeDtypeStruct((2, nc * ZROWS, 128), F32)),
        in_specs=[hbm] * 7,
        out_specs=(hbm, vmem),
        scratch_shapes=[
            pltpu.VMEM((1, 2, ROWS, LON), BF16),
            pltpu.VMEM((2, ROWS, LON), BF16),
            pltpu.VMEM((1,), F32),
            pltpu.VMEM((HK,), jnp.int32),
            pltpu.VMEM((1, 2, ROWS, LON), BF16),
            pltpu.VMEM((2, 16, 512), F32),
            pltpu.VMEM((2, 16, 512), BF16),
            pltpu.VMEM((2, 16, 512), BF16),
            pltpu.VMEM((2, ROWS, LON), F32),
            pltpu.VMEM((2, ROWS, LON), F32),
            pltpu.VMEM((4 * HK, WAVE), BF16),
            pltpu.VMEM((128, ROWS * 128), BF16),
            pltpu.VMEM((ROWS, HK, K + 1), BF16),
            pltpu.VMEM((64, WAVE), BF16),
            pltpu.VMEM((64, WAVE), BF16),
            pltpu.VMEM((HK, HK), BF16),
            pltpu.VMEM((2, 2, HK, ROWS * 128), F32),
            pltpu.VMEM((HK, wide), BF16),
            pltpu.VMEM((160, wide), BF16),
            pltpu.VMEM((160, wide), BF16),
            pltpu.VMEM((160, wide), F32),
            pltpu.VMEM((nc, 128, 128), F32),
            pltpu.VMEM((nc, 3, 128, 128), BF16),
            pltpu.VMEM((nc, 3, 128, 128), BF16),
            pltpu.VMEM((nc, 128, 128), F32),
            pltpu.VMEM((nc, NZ // 2, ZROWS, 128), F32),
            pltpu.VMEM((nc, NZ // 2, ZROWS, 128), BF16),
            pltpu.VMEM((nc, NZ // 2, ZROWS, 128), BF16),
            pltpu.VMEM((nc * ZROWS, 128), BF16),
            pltpu.VMEM((8, nc * ZROWS, 128), BF16),
            pltpu.SemaphoreType.DMA((9 + ROWS,)),
            pltpu.SemaphoreType.DMA,
            pltpu.SemaphoreType.DMA((2, 2)),
            pltpu.SemaphoreType.DMA((2, nc)),
            pltpu.SemaphoreType.DMA((nc, 3)),
            pltpu.SemaphoreType.DMA((nc, 3)),
            pltpu.SemaphoreType.DMA((nc, NZ // 2)),
            pltpu.SemaphoreType.DMA((nc, NZ // 2)),
            pltpu.SemaphoreType.DMA((2, 8)),
            pltpu.SemaphoreType.DMA((2, 8)),
            pltpu.SemaphoreType.REGULAR((7,)),
        ],
        compiler_params=pltpu.CompilerParams(
            collective_id=0, has_side_effects=True, vmem_limit_bytes=56 * 2**20
        ),
        name="transform",
    )(
        air,
        kappa,
        thick,
        perm,
        jnp.asarray(fourier_table()),
        jnp.asarray(spread_tables()),
        table,
    )
    smooth, spectral = pl.pallas_call(
        finish,
        out_shape=(grid, jax.ShapeDtypeStruct((2, SLOTS, 2, K + 1), F32)),
        in_specs=[vmem, vmem],
        out_specs=(hbm, vmem),
        scratch_shapes=[pltpu.SemaphoreType.DMA],
        name="finish",
    )(smooth, field)
    return smooth, jnp.transpose(spectral, (0, 2, 1, 3))[None]


def solution(mesh):
    return jax.shard_map(
        on_device,
        mesh=mesh,
        in_specs=(
            P("lev", None, "band", None),
            P(None, "band", None),
            P("lev"),
            P("band", None, None),
            P(),
        ),
        out_specs=(P("lev", None, "band", None), P("lev", None, None, "band", None)),
        check_vma=False,
    )
```

```python
import math

import jax
import jax.numpy as jnp
import ml_dtypes
import numpy as np
from jax import lax
from jax.experimental import pallas as pl
from jax.experimental.pallas import tpu as pltpu
from jax.sharding import PartitionSpec as P

LON = 4096
FOLD = 4
WAVE = LON // FOLD
STEPS = 1024
K = 640
HK = K // 2
ROWS = 8
NZ = 16
SLOTS = 5
F32 = jnp.float32
BF16 = jnp.bfloat16
CHUNKS = (
    ((0, 0), (1, 0), (0, 1)),
    ((1, 1), (0, 2), (1, 2)),
    ((0, 3), (1, 3)),
    ((0, 4), (1, 4), (None, 5)),
)
PLACE = {tile: k for k, tile in enumerate(t for c in CHUNKS for t in c)}
START = tuple(128 * PLACE[c[0]] for c in CHUNKS)
ZROWS = 16
TILES = len(PLACE)
LAST = 1
FAR = (4, 3, 5)
NEAR = (2, 6, 1, 7)


def fourier_table():
    p = np.arange(HK)
    m = np.concatenate([p, K - 1 - p])
    angle = (m[:, None] * np.arange(WAVE)[None, :] % LON) * (2.0 * math.pi / LON)
    table = np.concatenate([np.cos(angle), -np.sin(angle)], axis=0) / math.sqrt(LON)
    return table.astype(ml_dtypes.bfloat16)


def spread_tables():
    out = np.zeros((2, 4, 2, ROWS, ROWS, 128), np.float32)
    lane = np.arange(128)
    for group in range(4):
        odd_pair = 1 if group < 2 else 0
        for j in range(ROWS):
            out[:, group, 0, j, j] = 1.0
            out[0, group, 1, j, j] = 1.0 - 2.0 * (lane % 2)
            out[1, group, 1, j, j] = 1.0 - 2.0 * ((lane + odd_pair) % 2)
    return out.reshape(2 * 8 * ROWS, ROWS * 128).astype(ml_dtypes.bfloat16)


def nt(a, b):
    return lax.dot_general(a, b, (((1,), (1,)), ((), ())), preferred_element_type=F32)


def kernel(
    air_hbm, kappa_hbm, thick_hbm, perm_hbm, w_hbm, e_hbm, t_hbm,
    smooth_hbm, field,
    air, kappa, thick, perm, smooth,
    halo_rows, halo_send, halo_recv, base, x_base, w, e, t, xc, xs, onehot, coef, partial,
    core_send, core_recv, own, kept, quad_send, quad_recv, summed, packed, z_send, z_recv,
    lev_send, lev_recv,
    in_sem, out_sem, halo_sem, core_sem, qs_sem, qr_sem, zs_sem, zr_sem, ls_sem, lr_sem, told,
):
    band = lax.axis_index("band")
    lev = lax.axis_index("lev")
    z, xlo, core = band // 4, (band // 2) % 2, band % 2

    def at(zz, xx, cc, ll):
        return ((zz * 2 + xx) * 2 + cc, ll)

    yy, xhi = lev // 2, lev % 2
    core_peer = at(z, xlo, 1 - core, lev)
    pair_z = z + 1 - 2 * (z % 2)
    quad_peer = (
        at(pair_z, 1 - xlo, core, lev),
        at(z, 1 - xlo, core, lev),
        at(pair_z, xlo, core, lev),
    )
    z_peer = {d: at((z + d) % NZ, xlo, core, lev) for d in range(1, NZ)}
    lev_peer = {d: at(z, xlo, core, (lev + 8 - d) % 8) for d in range(1, 8)}
    y_peer = {d: at(z, xlo, core, ((yy + d) % 4) * 2 + xhi) for d in (1, 3)}
    far_x_peer = at(z, xlo, core, yy * 2 + 1 - xhi)
    halo_peer = (((band + 1) % 64, lev), ((band + 63) % 64, lev))
    mesh_id = pl.DeviceIdType.MESH

    barrier = pltpu.get_barrier_semaphore()
    peers = [
        *halo_peer, *quad_peer, z_peer[2], z_peer[14], y_peer[1], y_peer[3], far_x_peer,
    ]
    for peer in peers:
        pl.semaphore_signal(barrier, inc=1, device_id=peer, device_id_type=mesh_id)

    def tell(k, peer):
        pl.semaphore_signal(
            told.at[k], inc=1, device_id=peer, device_id_type=mesh_id
        )

    def heard(*ks):
        for k in ks:
            pl.semaphore_wait(told.at[k], 1)

    loads = [
        pltpu.make_async_copy(src, dst, in_sem.at[n])
        for n, (src, dst) in enumerate(
            [(air_hbm, air), (kappa_hbm, kappa), (perm_hbm, perm)]
            + [
                (w_hbm.at[pl.ds(k * HK, HK)], w.at[pl.ds(k * HK, HK)])
                for k in (0, 2, 1, 3)
            ]
            + [(e_hbm, e)]
            + [(thick_hbm, thick)]
            + [(t_hbm.at[k], t.at[k]) for k in range(ROWS)]
        )
    ]
    for load in loads:
        load.start()
    packed[...] = jnp.zeros_like(packed)

    row = lax.broadcasted_iota(jnp.int32, (ROWS, 1), 0)
    loads[0].wait()
    for hem in range(2):
        base[hem] = air[0, hem].astype(F32)
    for way, r in enumerate((ROWS - 1, 0)):
        for hem in range(2):
            for k in range(8):
                halo_rows[way, 8 * hem + k : 8 * hem + k + 1, :] = base[
                    hem, r : r + 1, 512 * k : 512 * k + 512
                ]
        halo_send[way] = halo_rows[way].astype(BF16)
    pl.semaphore_wait(barrier, len(peers))
    halo_copy = [
        pltpu.make_async_remote_copy(
            src_ref=halo_send.at[way],
            dst_ref=halo_recv.at[way],
            send_sem=halo_sem.at[0, way],
            recv_sem=halo_sem.at[1, way],
            device_id=halo_peer[way],
            device_id_type=mesh_id,
        )
        for way in range(2)
    ]
    for copy in halo_copy:
        copy.start()
    tell(0, z_peer[2])
    tell(1, z_peer[14])
    tell(5, y_peer[1])
    tell(6, y_peer[3])
    j = (band * ROWS + row).astype(F32)
    step = math.pi / STEPS
    centre = jnp.sin((j + 0.5) * step)
    upper = jnp.sin((j + 1.0) * step) / centre
    lower = jnp.sin(j * step) / centre
    last = band == 63
    loads[1].wait()
    for hem in range(2):
        u = base[hem]
        across = base[1 - hem][ROWS - 1 :, :]
        prev = jnp.where(row == 0, 0.0, pltpu.roll(u, 1, 0))
        succ = jnp.where(
            row == ROWS - 1, jnp.where(last, across, 0.0), pltpu.roll(u, ROWS - 1, 0)
        )
        east = pltpu.roll(u, LON - 1, 1)
        west = pltpu.roll(u, 1, 1)
        merid = upper * (succ - u) - lower * (u - prev)
        x_base[hem] = u + kappa[hem].astype(F32) * (east - 2.0 * u + west + merid)

    loads[2].wait()
    r = lax.broadcasted_iota(jnp.int32, (HK, HK), 0)
    col = lax.broadcasted_iota(jnp.int32, (HK, HK), 1)
    group = (r * 205) >> 10
    dz, dp, dx, dc = group & 7, (group >> 3) & 1, (group >> 4) & 1, group >> 5
    to_z = (jnp.where(dp == 0, pair_z, z) + 2 * dz) & 15
    to_x = jnp.where(dx == 0, 1 - xlo, xlo)
    to_c = jnp.where(dc == 0, 1 - core, core)
    slot = ((to_z * 2 + to_x) * 2 + to_c) * SLOTS + (r - 5 * group)
    order = jnp.where(slot == col, 1.0, 0.0).astype(BF16)
    pair_of = jnp.where(r == perm[...].reshape(1, HK), 1.0, 0.0).astype(BF16)
    onehot[...] = nt(order, pair_of).astype(BF16)

    heard(0, 1, 5, 6)
    tell(2, z_peer[4])
    tell(3, z_peer[12])
    tell(4, far_x_peer)

    folded = []
    for way in range(2):
        halo_copy[way].wait_recv()
        halo_rows[way] = halo_recv[way].astype(F32)
    for hem in range(2):
        pole, beyond = (
            jnp.concatenate(
                [halo_rows[way, 8 * hem + k : 8 * hem + k + 1, :] for k in range(8)],
                axis=1,
            )
            for way in range(2)
        )
        at_pole = jnp.where((row == 0) & (band > 0), lower, 0.0)
        at_edge = jnp.where((row == ROWS - 1) & (band < 63), upper, 0.0)
        s = x_base[hem] + kappa[hem].astype(F32) * (at_pole * pole + at_edge * beyond)
        s = s.astype(BF16)
        smooth[0, hem] = s
        folded.append(s.astype(F32))
    save = pltpu.make_async_copy(smooth, smooth_hbm, out_sem)
    save.start()
    q0, q1, q2, q3 = (
        jnp.concatenate([s[:, WAVE * k : WAVE * k + WAVE] for s in folded], axis=0)
        for k in range(FOLD)
    )
    even, odd = q0 + q2, q1 + q3
    y0, y2 = (even + odd).astype(BF16), (even - odd).astype(BF16)
    d02, d13 = (q0 - q2).astype(BF16), (q1 - q3).astype(BF16)
    for k, (c, d) in enumerate(((y0, y0), (y2, y2), (d02, d13), (d13, d02))):
        xc[pl.ds(16 * k, 16), :] = c
        xs[pl.ds(16 * k, 16), :] = d

    pairs = lax.broadcasted_iota(jnp.int32, (HK, 64), 0)
    group = lax.broadcasted_iota(jnp.int32, (HK, 64), 1) >> 4
    loads[7].wait()
    def fourier(back, carry):
        m = jnp.where(back == 1, K - 1 - pairs, pairs) & 3
        for k in range(2):
            pltpu.make_async_copy(
                w_hbm.at[pl.ds(0, HK)], w.at[pl.ds(0, HK)], in_sem.at[3 + 2 * back + k]
            ).wait()
        first = pl.multiple_of(back * HK, HK)
        cosine = nt(w[pl.ds(first, HK), :], xc[...])
        sine = nt(w[pl.ds(K + first, HK), :], xs[...])
        turn = jnp.where(m == 1, 1.0, -1.0)
        real = cosine + jnp.where(group == 2, turn * sine, 0.0)
        imag = sine - jnp.where(group == 3, turn * cosine, 0.0)
        odd = (m & 1) == 1
        for part, (f, g) in enumerate(((real, 2), (imag, 3))):
            keep = group == jnp.where(odd, g, m >> 1)
            coef[back, part] = jnp.dot(
                jnp.where(keep, f, 0.0).astype(BF16),
                e[pl.ds(pl.multiple_of(64 * back, 64), 64), :],
                preferred_element_type=F32,
            )
        return carry

    lax.fori_loop(0, 2, fourier, 0)
    for load in loads[8:]:
        load.wait()

    def kind_of(q, block):
        if q == 5:
            return "x"
        if 16 * block + 15 < K - 127 - 128 * q:
            return "a"
        return "b" if 16 * block >= K - 128 * q else "ab"

    def legendre(qs, first, count):
        kinds = [kind_of(q, first) for q in qs]
        lane = lax.broadcasted_iota(jnp.int32, (16, 128), 1)
        sub = lax.broadcasted_iota(jnp.int32, (16, 128), 0)

        def block(p0):
            rows = pl.ds(p0, 16)
            acc = [[0.0, 0.0] for _ in qs]
            front = [128 * q + lane < K - p0 - sub for q in qs]
            for jj in range(ROWS):
                cols = pl.ds(128 * jj, 128)
                ca = cb = None
                if "a" in kinds or "ab" in kinds:
                    ca = [coef[0, part, rows, cols] for part in range(2)]
                if "b" in kinds or "ab" in kinds or "x" in kinds:
                    cb = [coef[1, part, rows, cols] for part in range(2)]
                for n, (q, kind) in enumerate(zip(qs, kinds)):
                    if kind == "x":
                        tt = t[jj, rows, K : K + 1].astype(F32)
                    else:
                        tt = t[jj, rows, 128 * q : 128 * q + 128].astype(F32)
                    for part in range(2):
                        if kind == "a":
                            c = ca[part]
                        elif kind == "ab":
                            c = jnp.where(front[n], ca[part], cb[part])
                        elif kind == "b":
                            c = cb[part]
                        else:
                            c = cb[part][:, :1]
                        acc[n][part] = acc[n][part] + c * tt
            for n, (q, kind) in enumerate(zip(qs, kinds)):
                if kind == "x":
                    both = jnp.where(lane < LAST, acc[n][0], acc[n][1])
                    place = 128 * PLACE[None, q]
                    partial[rows, place : place + 128] = both.astype(BF16)
                else:
                    for part in range(2):
                        place = 128 * PLACE[part, q]
                        partial[rows, place : place + 128] = acc[n][part].astype(BF16)

        def body(i, carry):
            for n in range(2):
                block(pl.multiple_of((first + 2 * i + n) * 16, 16))
            return carry

        lax.fori_loop(0, count // 2, body, 0)

    def sums_of(*qs):
        first = 0
        for block in range(1, HK // 16 + 1):
            if block == HK // 16 or any(
                kind_of(q, block) != kind_of(q, first) for q in qs
            ):
                legendre(qs, first, block - first)
                first = block

    core_copy, quad_copy, z_copy = {}, {}, {}
    offset = START

    def core_step(c):
        n = 128 * len(CHUNKS[c])
        cols = slice(offset[c], offset[c] + n)
        mine = partial[:, cols]
        core_send[:, cols] = jnp.dot(
            onehot[pl.ds(0, 160), :], mine, preferred_element_type=F32
        ).astype(BF16)
        core_copy[c] = pltpu.make_async_remote_copy(
            src_ref=core_send.at[:, cols],
            dst_ref=core_recv.at[:, cols],
            send_sem=core_sem.at[0, c],
            recv_sem=core_sem.at[1, c],
            device_id=core_peer,
            device_id_type=mesh_id,
        )
        core_copy[c].start()
        own[:, cols] = jnp.dot(
            onehot[pl.ds(160, 160), :], mine, preferred_element_type=F32
        )

    def quad_step(c):
        count = len(CHUNKS[c])
        cols = slice(offset[c], offset[c] + 128 * count)
        core_copy[c].wait_recv()
        both = own[:, cols] + core_recv[:, cols].astype(F32)
        parts = [
            [both[40 * g : 40 * g + 40, 128 * n : 128 * n + 128] for n in range(count)]
            for g in range(4)
        ]
        quad_copy[c] = []
        for g in range(3):
            pad = [] if count == 2 else [jnp.zeros((8, 128), F32)]
            rows = pl.ds(0, 40 * count + 8 * len(pad))
            quad_send[c, g, rows, :] = jnp.concatenate(parts[g] + pad, axis=0).astype(
                BF16
            )
            copy = pltpu.make_async_remote_copy(
                src_ref=quad_send.at[c, g, rows],
                dst_ref=quad_recv.at[c, g, rows],
                send_sem=qs_sem.at[c, g],
                recv_sem=qr_sem.at[c, g],
                device_id=quad_peer[g],
                device_id_type=mesh_id,
            )
            copy.start()
            quad_copy[c].append(copy)
        kept[c, pl.ds(0, 40 * count), :] = jnp.concatenate(parts[3], axis=0)

    def z_step(c):
        count = len(CHUNKS[c])
        rows = 40 * count
        total = kept[c, pl.ds(0, rows), :]
        size = rows + (8 if count == 3 else 0)
        for g in range(3):
            quad_copy[c][g].wait_recv()
            total = total + quad_recv[c, g, pl.ds(0, size), :].astype(F32)[:rows, :]
        summed[c, pl.ds(0, rows), :] = total
        for d in range(NZ // 2):
            for n in range(count):
                packed[c, d, 5 * n : 5 * n + 5, :] = summed[
                    c, 40 * n + 5 * d : 40 * n + 5 * d + 5, :
                ]
        if c == 0:
            heard(2, 3, 4)
        for d in range(1, NZ // 2):
            z_send[c, d] = packed[c, d].astype(BF16)
        z_copy[c] = []
        send_z(c, FAR)

    def send_z(c, steps):
        for d in steps:
            copy = pltpu.make_async_remote_copy(
                src_ref=z_send.at[c, d],
                dst_ref=z_recv.at[c, d],
                send_sem=zs_sem.at[c, d],
                recv_sem=zr_sem.at[c, d],
                device_id=z_peer[2 * d],
                device_id_type=mesh_id,
            )
            copy.start()
            z_copy[c].append(copy)

    sums_of(0, 1)
    core_step(0)
    sums_of(2)
    core_step(1)
    quad_step(0)
    sums_of(3)
    core_step(2)
    quad_step(1)
    sums_of(4, 5)
    core_step(3)
    quad_step(2)
    quad_step(3)
    z_step(0)
    z_step(1)
    z_step(2)
    z_step(3)
    for c in range(len(CHUNKS)):
        send_z(c, NEAR)

    thickness = thick[...].reshape(1, 1)
    for copy in halo_copy:
        copy.wait_send()
    half = len(CHUNKS) // 2 * ZROWS
    lev_copy = {}
    for c in range(len(CHUNKS)):
        for copy in z_copy[c]:
            copy.wait_recv()
        total = packed[c, 0]
        for d in range(1, NZ // 2):
            total = total + z_recv[c, d].astype(F32)
        rows = pl.ds(ZROWS * c, ZROWS)
        total_w = total * thickness
        lev_send[rows, :] = total_w.astype(BF16)
        field[0, rows, :] = total
        field[1, rows, :] = 0.5 * total_w
        if c % 2:
            h = c // 2
            part = pl.ds(half * h, half)
            for d in range(7, 0, -1):
                lev_copy[h, d] = pltpu.make_async_remote_copy(
                    src_ref=lev_send.at[part],
                    dst_ref=lev_recv.at[d, part],
                    send_sem=ls_sem.at[h, d],
                    recv_sem=lr_sem.at[h, d],
                    device_id=lev_peer[d],
                    device_id_type=mesh_id,
                )

                @pl.when(lev >= d)
                def _():
                    lev_copy[h, d].start()

    for d in range(1, 8):

        @pl.when(lev + d < 8)
        def _():
            lev_copy[0, d].wait_recv()
            lev_copy[1, d].wait_recv()
            field[1] += lev_recv[d].astype(F32)

    save.wait()
    for c in range(len(CHUNKS)):
        core_copy[c].wait_send()
        for copy in quad_copy[c] + z_copy[c]:
            copy.wait_send()
    for d in range(1, 8):

        @pl.when(lev >= d)
        def _():
            lev_copy[0, d].wait_send()
            lev_copy[1, d].wait_send()


def finish(smooth_in, field, smooth_out, spectral, sem):
    copy = pltpu.make_async_copy(smooth_in, smooth_out, sem)
    copy.start()
    for f in range(2):
        for c, tiles in enumerate(CHUNKS):
            for n, (part, q) in enumerate(tiles):
                for i in range(SLOTS):
                    k = ZROWS * c + 5 * n + i
                    if part is None:
                        for half in range(2):
                            spectral[f, i, half : half + 1, K : K + 1] = field[
                                f, k : k + 1, LAST * half : LAST * half + 1
                            ]
                    else:
                        spectral[f, i, part : part + 1, 128 * q : 128 * q + 128] = (
                            field[f, k : k + 1, :]
                        )
    copy.wait()


def on_device(air, kappa, thick, table, perm):
    vmem = pl.BlockSpec(memory_space=pltpu.VMEM)
    hbm = pl.BlockSpec(memory_space=pl.ANY)
    nc = len(CHUNKS)
    wide = 128 * TILES
    grid = jax.ShapeDtypeStruct((1, 2, ROWS, LON), BF16)
    smooth, field = pl.pallas_call(
        kernel,
        out_shape=(grid, jax.ShapeDtypeStruct((2, nc * ZROWS, 128), F32)),
        in_specs=[hbm] * 7,
        out_specs=(hbm, vmem),
        scratch_shapes=[
            pltpu.VMEM((1, 2, ROWS, LON), BF16),
            pltpu.VMEM((2, ROWS, LON), BF16),
            pltpu.VMEM((1,), F32),
            pltpu.VMEM((HK,), jnp.int32),
            pltpu.VMEM((1, 2, ROWS, LON), BF16),
            pltpu.VMEM((2, 16, 512), F32),
            pltpu.VMEM((2, 16, 512), BF16),
            pltpu.VMEM((2, 16, 512), BF16),
            pltpu.VMEM((2, ROWS, LON), F32),
            pltpu.VMEM((2, ROWS, LON), F32),
            pltpu.VMEM((4 * HK, WAVE), BF16),
            pltpu.VMEM((128, ROWS * 128), BF16),
            pltpu.VMEM((ROWS, HK, K + 1), BF16),
            pltpu.VMEM((64, WAVE), BF16),
            pltpu.VMEM((64, WAVE), BF16),
            pltpu.VMEM((HK, HK), BF16),
            pltpu.VMEM((2, 2, HK, ROWS * 128), F32),
            pltpu.VMEM((HK, wide), BF16),
            pltpu.VMEM((160, wide), BF16),
            pltpu.VMEM((160, wide), BF16),
            pltpu.VMEM((160, wide), F32),
            pltpu.VMEM((nc, 128, 128), F32),
            pltpu.VMEM((nc, 3, 128, 128), BF16),
            pltpu.VMEM((nc, 3, 128, 128), BF16),
            pltpu.VMEM((nc, 128, 128), F32),
            pltpu.VMEM((nc, NZ // 2, ZROWS, 128), F32),
            pltpu.VMEM((nc, NZ // 2, ZROWS, 128), BF16),
            pltpu.VMEM((nc, NZ // 2, ZROWS, 128), BF16),
            pltpu.VMEM((nc * ZROWS, 128), BF16),
            pltpu.VMEM((8, nc * ZROWS, 128), BF16),
            pltpu.SemaphoreType.DMA((9 + ROWS,)),
            pltpu.SemaphoreType.DMA,
            pltpu.SemaphoreType.DMA((2, 2)),
            pltpu.SemaphoreType.DMA((2, nc)),
            pltpu.SemaphoreType.DMA((nc, 3)),
            pltpu.SemaphoreType.DMA((nc, 3)),
            pltpu.SemaphoreType.DMA((nc, NZ // 2)),
            pltpu.SemaphoreType.DMA((nc, NZ // 2)),
            pltpu.SemaphoreType.DMA((2, 8)),
            pltpu.SemaphoreType.DMA((2, 8)),
            pltpu.SemaphoreType.REGULAR((7,)),
        ],
        compiler_params=pltpu.CompilerParams(
            collective_id=0, has_side_effects=True, vmem_limit_bytes=56 * 2**20
        ),
        name="transform",
    )(
        air,
        kappa,
        thick,
        perm,
        jnp.asarray(fourier_table()),
        jnp.asarray(spread_tables()),
        table,
    )
    smooth, spectral = pl.pallas_call(
        finish,
        out_shape=(grid, jax.ShapeDtypeStruct((2, SLOTS, 2, K + 1), F32)),
        in_specs=[vmem, vmem],
        out_specs=(hbm, vmem),
        scratch_shapes=[pltpu.SemaphoreType.DMA],
        name="finish",
    )(smooth, field)
    return smooth, jnp.transpose(spectral, (0, 2, 1, 3))[None]


def solution(mesh):
    return jax.shard_map(
        on_device,
        mesh=mesh,
        in_specs=(
            P("lev", None, "band", None),
            P(None, "band", None),
            P("lev"),
            P("band", None, None),
            P(),
        ),
        out_specs=(P("lev", None, "band", None), P("lev", None, None, "band", None)),
        check_vma=False,
    )
```

```python
import math

import jax
import jax.numpy as jnp
import ml_dtypes
import numpy as np
from jax import lax
from jax.experimental import pallas as pl
from jax.experimental.pallas import tpu as pltpu
from jax.sharding import PartitionSpec as P

LON = 4096
FOLD = 4
WAVE = LON // FOLD
STEPS = 1024
K = 640
HK = K // 2
ROWS = 8
NZ = 16
SLOTS = 5
F32 = jnp.float32
BF16 = jnp.bfloat16
CHUNKS = (
    ((0, 0), (1, 0), (0, 1)),
    ((1, 1), (0, 2), (1, 2)),
    ((0, 3), (1, 3), (None, 5)),
    ((0, 4), (1, 4)),
)
PLACE = {tile: k for k, tile in enumerate(t for c in CHUNKS for t in c)}
START = tuple(128 * PLACE[c[0]] for c in CHUNKS)
ZROWS = 16
TILES = len(PLACE)
LAST = 1
FAR = (4, 3, 5)
NEAR = (2, 6, 1, 7)


def fourier_table():
    p = np.arange(HK)
    m = np.concatenate([p, K - 1 - p])
    angle = (m[:, None] * np.arange(WAVE)[None, :] % LON) * (2.0 * math.pi / LON)
    table = np.concatenate([np.cos(angle), -np.sin(angle)], axis=0) / math.sqrt(LON)
    return table.astype(ml_dtypes.bfloat16)


def spread_tables():
    out = np.zeros((2, 4, 2, ROWS, ROWS, 128), np.float32)
    lane = np.arange(128)
    for group in range(4):
        odd_pair = 1 if group < 2 else 0
        for j in range(ROWS):
            out[:, group, 0, j, j] = 1.0
            out[0, group, 1, j, j] = 1.0 - 2.0 * (lane % 2)
            out[1, group, 1, j, j] = 1.0 - 2.0 * ((lane + odd_pair) % 2)
    return out.reshape(2 * 8 * ROWS, ROWS * 128).astype(ml_dtypes.bfloat16)


def nt(a, b):
    return lax.dot_general(a, b, (((1,), (1,)), ((), ())), preferred_element_type=F32)


def kernel(
    air_hbm, kappa_hbm, thick_hbm, perm_hbm, w_hbm, e_hbm, t_hbm,
    smooth_hbm, field,
    air, kappa, thick, perm, smooth,
    halo_rows, halo_send, halo_recv, base, x_base, w, e, t, xc, xs, onehot, coef, partial,
    core_send, core_recv, own, kept, quad_send, quad_recv, summed, packed, z_send, z_recv,
    lev_send, lev_recv,
    in_sem, out_sem, halo_sem, core_sem, qs_sem, qr_sem, zs_sem, zr_sem, ls_sem, lr_sem, told,
):
    band = lax.axis_index("band")
    lev = lax.axis_index("lev")
    z, xlo, core = band // 4, (band // 2) % 2, band % 2

    def at(zz, xx, cc, ll):
        return ((zz * 2 + xx) * 2 + cc, ll)

    yy, xhi = lev // 2, lev % 2
    core_peer = at(z, xlo, 1 - core, lev)
    pair_z = z + 1 - 2 * (z % 2)
    quad_peer = (
        at(pair_z, 1 - xlo, core, lev),
        at(z, 1 - xlo, core, lev),
        at(pair_z, xlo, core, lev),
    )
    z_peer = {d: at((z + d) % NZ, xlo, core, lev) for d in range(1, NZ)}
    lev_peer = {d: at(z, xlo, core, (lev + 8 - d) % 8) for d in range(1, 8)}
    y_peer = {d: at(z, xlo, core, ((yy + d) % 4) * 2 + xhi) for d in (1, 3)}
    far_x_peer = at(z, xlo, core, yy * 2 + 1 - xhi)
    halo_peer = (((band + 1) % 64, lev), ((band + 63) % 64, lev))
    mesh_id = pl.DeviceIdType.MESH

    barrier = pltpu.get_barrier_semaphore()
    peers = [
        *halo_peer, *quad_peer, z_peer[2], z_peer[14], y_peer[1], y_peer[3], far_x_peer,
    ]
    for peer in peers:
        pl.semaphore_signal(barrier, inc=1, device_id=peer, device_id_type=mesh_id)

    def tell(k, peer):
        pl.semaphore_signal(
            told.at[k], inc=1, device_id=peer, device_id_type=mesh_id
        )

    def heard(*ks):
        for k in ks:
            pl.semaphore_wait(told.at[k], 1)

    loads = [
        pltpu.make_async_copy(src, dst, in_sem.at[n])
        for n, (src, dst) in enumerate(
            [(air_hbm, air), (kappa_hbm, kappa), (perm_hbm, perm)]
            + [
                (w_hbm.at[pl.ds(k * HK, HK)], w.at[pl.ds(k * HK, HK)])
                for k in (0, 2, 1, 3)
            ]
            + [(e_hbm, e)]
            + [(thick_hbm, thick)]
            + [(t_hbm.at[k], t.at[k]) for k in range(ROWS)]
        )
    ]
    for load in loads:
        load.start()
    packed[...] = jnp.zeros_like(packed)

    row = lax.broadcasted_iota(jnp.int32, (ROWS, 1), 0)
    loads[0].wait()
    for hem in range(2):
        base[hem] = air[0, hem].astype(F32)
    for way, r in enumerate((ROWS - 1, 0)):
        for hem in range(2):
            for k in range(8):
                halo_rows[way, 8 * hem + k : 8 * hem + k + 1, :] = base[
                    hem, r : r + 1, 512 * k : 512 * k + 512
                ]
        halo_send[way] = halo_rows[way].astype(BF16)
    pl.semaphore_wait(barrier, len(peers))
    halo_copy = [
        pltpu.make_async_remote_copy(
            src_ref=halo_send.at[way],
            dst_ref=halo_recv.at[way],
            send_sem=halo_sem.at[0, way],
            recv_sem=halo_sem.at[1, way],
            device_id=halo_peer[way],
            device_id_type=mesh_id,
        )
        for way in range(2)
    ]
    for copy in halo_copy:
        copy.start()
    tell(0, z_peer[2])
    tell(1, z_peer[14])
    tell(5, y_peer[1])
    tell(6, y_peer[3])
    j = (band * ROWS + row).astype(F32)
    step = math.pi / STEPS
    centre = jnp.sin((j + 0.5) * step)
    upper = jnp.sin((j + 1.0) * step) / centre
    lower = jnp.sin(j * step) / centre
    last = band == 63
    loads[1].wait()
    for hem in range(2):
        u = base[hem]
        across = base[1 - hem][ROWS - 1 :, :]
        prev = jnp.where(row == 0, 0.0, pltpu.roll(u, 1, 0))
        succ = jnp.where(
            row == ROWS - 1, jnp.where(last, across, 0.0), pltpu.roll(u, ROWS - 1, 0)
        )
        east = pltpu.roll(u, LON - 1, 1)
        west = pltpu.roll(u, 1, 1)
        merid = upper * (succ - u) - lower * (u - prev)
        x_base[hem] = u + kappa[hem].astype(F32) * (east - 2.0 * u + west + merid)

    loads[2].wait()
    r = lax.broadcasted_iota(jnp.int32, (HK, HK), 0)
    col = lax.broadcasted_iota(jnp.int32, (HK, HK), 1)
    group = (r * 205) >> 10
    dz, dp, dx, dc = group & 7, (group >> 3) & 1, (group >> 4) & 1, group >> 5
    to_z = (jnp.where(dp == 0, pair_z, z) + 2 * dz) & 15
    to_x = jnp.where(dx == 0, 1 - xlo, xlo)
    to_c = jnp.where(dc == 0, 1 - core, core)
    slot = ((to_z * 2 + to_x) * 2 + to_c) * SLOTS + (r - 5 * group)
    order = jnp.where(slot == col, 1.0, 0.0).astype(BF16)
    pair_of = jnp.where(r == perm[...].reshape(1, HK), 1.0, 0.0).astype(BF16)
    onehot[...] = nt(order, pair_of).astype(BF16)

    heard(0, 1, 5, 6)
    tell(2, z_peer[4])
    tell(3, z_peer[12])
    tell(4, far_x_peer)

    folded = []
    for way in range(2):
        halo_copy[way].wait_recv()
        halo_rows[way] = halo_recv[way].astype(F32)
    for hem in range(2):
        pole, beyond = (
            jnp.concatenate(
                [halo_rows[way, 8 * hem + k : 8 * hem + k + 1, :] for k in range(8)],
                axis=1,
            )
            for way in range(2)
        )
        at_pole = jnp.where((row == 0) & (band > 0), lower, 0.0)
        at_edge = jnp.where((row == ROWS - 1) & (band < 63), upper, 0.0)
        s = x_base[hem] + kappa[hem].astype(F32) * (at_pole * pole + at_edge * beyond)
        s = s.astype(BF16)
        smooth[0, hem] = s
        folded.append(s.astype(F32))
    save = pltpu.make_async_copy(smooth, smooth_hbm, out_sem)
    save.start()
    q0, q1, q2, q3 = (
        jnp.concatenate([s[:, WAVE * k : WAVE * k + WAVE] for s in folded], axis=0)
        for k in range(FOLD)
    )
    even, odd = q0 + q2, q1 + q3
    y0, y2 = (even + odd).astype(BF16), (even - odd).astype(BF16)
    d02, d13 = (q0 - q2).astype(BF16), (q1 - q3).astype(BF16)
    for k, (c, d) in enumerate(((y0, y0), (y2, y2), (d02, d13), (d13, d02))):
        xc[pl.ds(16 * k, 16), :] = c
        xs[pl.ds(16 * k, 16), :] = d

    pairs = lax.broadcasted_iota(jnp.int32, (HK, 64), 0)
    group = lax.broadcasted_iota(jnp.int32, (HK, 64), 1) >> 4
    loads[7].wait()
    def fourier(back, carry):
        m = jnp.where(back == 1, K - 1 - pairs, pairs) & 3
        for k in range(2):
            pltpu.make_async_copy(
                w_hbm.at[pl.ds(0, HK)], w.at[pl.ds(0, HK)], in_sem.at[3 + 2 * back + k]
            ).wait()
        first = pl.multiple_of(back * HK, HK)
        cosine = nt(w[pl.ds(first, HK), :], xc[...])
        sine = nt(w[pl.ds(K + first, HK), :], xs[...])
        turn = jnp.where(m == 1, 1.0, -1.0)
        real = cosine + jnp.where(group == 2, turn * sine, 0.0)
        imag = sine - jnp.where(group == 3, turn * cosine, 0.0)
        odd = (m & 1) == 1
        for part, (f, g) in enumerate(((real, 2), (imag, 3))):
            keep = group == jnp.where(odd, g, m >> 1)
            coef[back, part] = jnp.dot(
                jnp.where(keep, f, 0.0).astype(BF16),
                e[pl.ds(pl.multiple_of(64 * back, 64), 64), :],
                preferred_element_type=F32,
            )
        return carry

    lax.fori_loop(0, 2, fourier, 0)
    for load in loads[8:]:
        load.wait()

    def kind_of(q, block):
        if q == 5:
            return "x"
        if 16 * block + 15 < K - 127 - 128 * q:
            return "a"
        return "b" if 16 * block >= K - 128 * q else "ab"

    def legendre(qs, first, count):
        kinds = [kind_of(q, first) for q in qs]
        lane = lax.broadcasted_iota(jnp.int32, (16, 128), 1)
        sub = lax.broadcasted_iota(jnp.int32, (16, 128), 0)

        def block(p0):
            rows = pl.ds(p0, 16)
            acc = [[0.0, 0.0] for _ in qs]
            front = [128 * q + lane < K - p0 - sub for q in qs]
            for jj in range(ROWS):
                cols = pl.ds(128 * jj, 128)
                ca = cb = None
                if "a" in kinds or "ab" in kinds:
                    ca = [coef[0, part, rows, cols] for part in range(2)]
                if "b" in kinds or "ab" in kinds or "x" in kinds:
                    cb = [coef[1, part, rows, cols] for part in range(2)]
                for n, (q, kind) in enumerate(zip(qs, kinds)):
                    if kind == "x":
                        tt = t[jj, rows, K : K + 1].astype(F32)
                    else:
                        tt = t[jj, rows, 128 * q : 128 * q + 128].astype(F32)
                    for part in range(2):
                        if kind == "a":
                            c = ca[part]
                        elif kind == "ab":
                            c = jnp.where(front[n], ca[part], cb[part])
                        elif kind == "b":
                            c = cb[part]
                        else:
                            c = cb[part][:, :1]
                        acc[n][part] = acc[n][part] + c * tt
            for n, (q, kind) in enumerate(zip(qs, kinds)):
                if kind == "x":
                    both = jnp.where(lane < LAST, acc[n][0], acc[n][1])
                    place = 128 * PLACE[None, q]
                    partial[rows, place : place + 128] = both.astype(BF16)
                else:
                    for part in range(2):
                        place = 128 * PLACE[part, q]
                        partial[rows, place : place + 128] = acc[n][part].astype(BF16)

        def body(i, carry):
            for n in range(2):
                block(pl.multiple_of((first + 2 * i + n) * 16, 16))
            return carry

        lax.fori_loop(0, count // 2, body, 0)

    def sums_of(*qs):
        first = 0
        for block in range(1, HK // 16 + 1):
            if block == HK // 16 or any(
                kind_of(q, block) != kind_of(q, first) for q in qs
            ):
                legendre(qs, first, block - first)
                first = block

    core_copy, quad_copy, z_copy = {}, {}, {}
    offset = START

    def core_step(c):
        n = 128 * len(CHUNKS[c])
        cols = slice(offset[c], offset[c] + n)
        mine = partial[:, cols]
        core_send[:, cols] = jnp.dot(
            onehot[pl.ds(0, 160), :], mine, preferred_element_type=F32
        ).astype(BF16)
        core_copy[c] = pltpu.make_async_remote_copy(
            src_ref=core_send.at[:, cols],
            dst_ref=core_recv.at[:, cols],
            send_sem=core_sem.at[0, c],
            recv_sem=core_sem.at[1, c],
            device_id=core_peer,
            device_id_type=mesh_id,
        )
        core_copy[c].start()
        own[:, cols] = jnp.dot(
            onehot[pl.ds(160, 160), :], mine, preferred_element_type=F32
        )

    def turned(tile):
        pad = jnp.zeros((128 - tile.shape[0], 128), F32)
        return jnp.transpose(jnp.concatenate([tile, pad], axis=0))

    def quad_step(c):
        count = len(CHUNKS[c])
        cols = slice(offset[c], offset[c] + 128 * count)
        core_copy[c].wait_recv()
        both = own[:, cols] + core_recv[:, cols].astype(F32)
        parts = [
            [both[40 * g : 40 * g + 40, 128 * n : 128 * n + 128] for n in range(count)]
            for g in range(4)
        ]
        quad_copy[c] = []
        for g in range(3):
            tiles = list(parts[g])
            if CHUNKS[c][-1][0] is None:
                tiles[-1] = turned(tiles[-1])[:8, :]
            if count == 3:
                tiles.append(jnp.zeros((8, 128), F32))
            tiles = jnp.concatenate(tiles, axis=0)
            rows = pl.ds(0, tiles.shape[0])
            quad_send[c, g, rows, :] = tiles.astype(BF16)
            copy = pltpu.make_async_remote_copy(
                src_ref=quad_send.at[c, g, rows],
                dst_ref=quad_recv.at[c, g, rows],
                send_sem=qs_sem.at[c, g],
                recv_sem=qr_sem.at[c, g],
                device_id=quad_peer[g],
                device_id_type=mesh_id,
            )
            copy.start()
            quad_copy[c].append(copy)
        kept[c, pl.ds(0, 40 * count), :] = jnp.concatenate(parts[3], axis=0)

    def z_step(c):
        count = len(CHUNKS[c])
        rows = 40 * count
        thin = CHUNKS[c][-1][0] is None
        size = 96 if thin else rows + (8 if count == 3 else 0)
        came = 0.0
        for g in range(3):
            quad_copy[c][g].wait_recv()
            came = came + quad_recv[c, g, pl.ds(0, size), :].astype(F32)
        if thin:
            came = jnp.concatenate([came[:80], turned(came[80:88])[:40]], axis=0)
        summed[c, pl.ds(0, rows), :] = kept[c, pl.ds(0, rows), :] + came[:rows]
        for d in range(NZ // 2):
            for n in range(count):
                packed[c, d, 5 * n : 5 * n + 5, :] = summed[
                    c, 40 * n + 5 * d : 40 * n + 5 * d + 5, :
                ]
        if c == 0:
            heard(2, 3, 4)
        for d in range(1, NZ // 2):
            z_send[c, d] = packed[c, d].astype(BF16)
        z_copy[c] = []
        send_z(c, FAR)

    def send_z(c, steps):
        for d in steps:
            copy = pltpu.make_async_remote_copy(
                src_ref=z_send.at[c, d],
                dst_ref=z_recv.at[c, d],
                send_sem=zs_sem.at[c, d],
                recv_sem=zr_sem.at[c, d],
                device_id=z_peer[2 * d],
                device_id_type=mesh_id,
            )
            copy.start()
            z_copy[c].append(copy)

    sums_of(0, 1)
    core_step(0)
    sums_of(2)
    core_step(1)
    quad_step(0)
    sums_of(3, 5)
    core_step(2)
    quad_step(1)
    sums_of(4)
    core_step(3)
    quad_step(2)
    quad_step(3)
    z_step(0)
    z_step(1)
    z_step(2)
    z_step(3)
    for c in range(len(CHUNKS)):
        send_z(c, NEAR)

    thickness = thick[...].reshape(1, 1)
    for copy in halo_copy:
        copy.wait_send()
    ends = len(CHUNKS) - 2, len(CHUNKS) - 1
    lev_copy = {}
    for c in range(len(CHUNKS)):
        for copy in z_copy[c]:
            copy.wait_recv()
        total = packed[c, 0]
        for d in range(1, NZ // 2):
            total = total + z_recv[c, d].astype(F32)
        rows = pl.ds(ZROWS * c, ZROWS)
        total_w = total * thickness
        lev_send[rows, :] = total_w.astype(BF16)
        field[0, rows, :] = total
        field[1, rows, :] = 0.5 * total_w
        if c in ends:
            h = ends.index(c)
            part = pl.ds(ZROWS * c, ZROWS) if h else pl.ds(0, ZROWS * (c + 1))
            for d in range(7, 0, -1):
                lev_copy[h, d] = pltpu.make_async_remote_copy(
                    src_ref=lev_send.at[part],
                    dst_ref=lev_recv.at[d, part],
                    send_sem=ls_sem.at[h, d],
                    recv_sem=lr_sem.at[h, d],
                    device_id=lev_peer[d],
                    device_id_type=mesh_id,
                )

                @pl.when(lev >= d)
                def _():
                    lev_copy[h, d].start()

    for d in range(1, 8):

        @pl.when(lev + d < 8)
        def _():
            lev_copy[0, d].wait_recv()
            lev_copy[1, d].wait_recv()
            field[1] += lev_recv[d].astype(F32)

    save.wait()
    for c in range(len(CHUNKS)):
        core_copy[c].wait_send()
        for copy in quad_copy[c] + z_copy[c]:
            copy.wait_send()
    for d in range(1, 8):

        @pl.when(lev >= d)
        def _():
            lev_copy[0, d].wait_send()
            lev_copy[1, d].wait_send()


def finish(smooth_in, field, smooth_out, spectral, sem):
    copy = pltpu.make_async_copy(smooth_in, smooth_out, sem)
    copy.start()
    for f in range(2):
        for c, tiles in enumerate(CHUNKS):
            for n, (part, q) in enumerate(tiles):
                for i in range(SLOTS):
                    k = ZROWS * c + 5 * n + i
                    if part is None:
                        for half in range(2):
                            spectral[f, i, half : half + 1, K : K + 1] = field[
                                f, k : k + 1, LAST * half : LAST * half + 1
                            ]
                    else:
                        spectral[f, i, part : part + 1, 128 * q : 128 * q + 128] = (
                            field[f, k : k + 1, :]
                        )
    copy.wait()


def on_device(air, kappa, thick, table, perm):
    vmem = pl.BlockSpec(memory_space=pltpu.VMEM)
    hbm = pl.BlockSpec(memory_space=pl.ANY)
    nc = len(CHUNKS)
    wide = 128 * TILES
    grid = jax.ShapeDtypeStruct((1, 2, ROWS, LON), BF16)
    smooth, field = pl.pallas_call(
        kernel,
        out_shape=(grid, jax.ShapeDtypeStruct((2, nc * ZROWS, 128), F32)),
        in_specs=[hbm] * 7,
        out_specs=(hbm, vmem),
        scratch_shapes=[
            pltpu.VMEM((1, 2, ROWS, LON), BF16),
            pltpu.VMEM((2, ROWS, LON), BF16),
            pltpu.VMEM((1,), F32),
            pltpu.VMEM((HK,), jnp.int32),
            pltpu.VMEM((1, 2, ROWS, LON), BF16),
            pltpu.VMEM((2, 16, 512), F32),
            pltpu.VMEM((2, 16, 512), BF16),
            pltpu.VMEM((2, 16, 512), BF16),
            pltpu.VMEM((2, ROWS, LON), F32),
            pltpu.VMEM((2, ROWS, LON), F32),
            pltpu.VMEM((4 * HK, WAVE), BF16),
            pltpu.VMEM((128, ROWS * 128), BF16),
            pltpu.VMEM((ROWS, HK, K + 1), BF16),
            pltpu.VMEM((64, WAVE), BF16),
            pltpu.VMEM((64, WAVE), BF16),
            pltpu.VMEM((HK, HK), BF16),
            pltpu.VMEM((2, 2, HK, ROWS * 128), F32),
            pltpu.VMEM((HK, wide), BF16),
            pltpu.VMEM((160, wide), BF16),
            pltpu.VMEM((160, wide), BF16),
            pltpu.VMEM((160, wide), F32),
            pltpu.VMEM((nc, 128, 128), F32),
            pltpu.VMEM((nc, 3, 128, 128), BF16),
            pltpu.VMEM((nc, 3, 128, 128), BF16),
            pltpu.VMEM((nc, 128, 128), F32),
            pltpu.VMEM((nc, NZ // 2, ZROWS, 128), F32),
            pltpu.VMEM((nc, NZ // 2, ZROWS, 128), BF16),
            pltpu.VMEM((nc, NZ // 2, ZROWS, 128), BF16),
            pltpu.VMEM((nc * ZROWS, 128), BF16),
            pltpu.VMEM((8, nc * ZROWS, 128), BF16),
            pltpu.SemaphoreType.DMA((9 + ROWS,)),
            pltpu.SemaphoreType.DMA,
            pltpu.SemaphoreType.DMA((2, 2)),
            pltpu.SemaphoreType.DMA((2, nc)),
            pltpu.SemaphoreType.DMA((nc, 3)),
            pltpu.SemaphoreType.DMA((nc, 3)),
            pltpu.SemaphoreType.DMA((nc, NZ // 2)),
            pltpu.SemaphoreType.DMA((nc, NZ // 2)),
            pltpu.SemaphoreType.DMA((2, 8)),
            pltpu.SemaphoreType.DMA((2, 8)),
            pltpu.SemaphoreType.REGULAR((7,)),
        ],
        compiler_params=pltpu.CompilerParams(
            collective_id=0, has_side_effects=True, vmem_limit_bytes=56 * 2**20
        ),
        name="transform",
    )(
        air,
        kappa,
        thick,
        perm,
        jnp.asarray(fourier_table()),
        jnp.asarray(spread_tables()),
        table,
    )
    smooth, spectral = pl.pallas_call(
        finish,
        out_shape=(grid, jax.ShapeDtypeStruct((2, SLOTS, 2, K + 1), F32)),
        in_specs=[vmem, vmem],
        out_specs=(hbm, vmem),
        scratch_shapes=[pltpu.SemaphoreType.DMA],
        name="finish",
    )(smooth, field)
    return smooth, jnp.transpose(spectral, (0, 2, 1, 3))[None]


def solution(mesh):
    return jax.shard_map(
        on_device,
        mesh=mesh,
        in_specs=(
            P("lev", None, "band", None),
            P(None, "band", None),
            P("lev"),
            P("band", None, None),
            P(),
        ),
        out_specs=(P("lev", None, "band", None), P("lev", None, None, "band", None)),
        check_vma=False,
    )
```
